32 devices in a mesh: seq: 8 (over z, x), kvh: 4 (over y, core).
Axes of the slice: x: 2, y: 2, z: 4, core: 2. Of those that a mesh axis runs over, the one named last changes fastest.
Arguments:
- queries: bfloat16 [2048, 2048], P('seq', 'kvh'), may hold values from -12 to 12
- kv_cache: bfloat16 [2, 65536, 512], P(None, 'seq', 'kvh'), may hold values from -6 to 6
- selected: int32 [16, 4, 2], P('seq', 'kvh'), may hold values from 0 to 62, as said below
- out_weight: bfloat16 [2048, 4096], P('kvh', 'seq'), may hold values from -0.1875 to 0.1875
Outputs:
- output: bfloat16 [2048, 4096], P('seq', 'kvh')
The draws below stay inside these ranges and needn't reach their ends.
Inputs may be any that keep to these rules, and one draw needn't show every extreme that they name: `selected`: for each KV head, the 4 blocks named by the tiles of one device of seq lie in the ranges of distinct devices (block b lies in the range of device b // 8); for each KV head, some device's range is named by a tile of every device.
All inputs are finite; a program needn't handle non-finite values.
Results may differ from the reference program's by a relative error of at most 0.017.
Values may be sent and summed in bfloat16 or wider, within the bound.
No kernel may reach another device: no remote copies, remote signals or barrier semaphores. Data moves between devices by JAX's collectives and lax.ppermute only.
A program may use at most 128 MiB of HBM per device.

```python
import jax
import jax.numpy as jnp
from jax import lax

GROUP = 4
HD = 128
DOUT = 4096
BLK = 1024
TILE = 128
SEL = 2
KVB_DEV = 8
QT_DEV = 256
KVH = 4
H = 16
TPD = 2
TILES = 16
QTOK = 2048
NB = 64


def draw_queries(key, part):
    noise_key = jax.random.fold_in(key, 11)
    return (jnp.clip(jax.random.normal(noise_key, (QTOK, H * HD), jnp.float32), -6.0, 6.0) * 2.0).astype(jnp.bfloat16)


def draw_kv_cache(key, part):
    noise_key = jax.random.fold_in(key, 13)
    return jnp.clip(jax.random.normal(noise_key, (2, NB * BLK, KVH * HD), jnp.float32), -6.0, 6.0).astype(jnp.bfloat16)


def draw_selected(key, part):
    devices = NB // KVB_DEV
    wanted = TPD * SEL
    base_key = jax.random.fold_in(key, 17)
    key_hot, key_favour, key_noise, key_order, key_first, key_second = jax.random.split(base_key, 6)
    hottest = jax.random.randint(key_hot, (KVH,), 0, devices)
    favour = jax.random.randint(key_favour, (devices,), 0, 4)
    noise = jax.random.randint(key_noise, (devices, KVH, devices), 0, 4096)
    owner_ids = jnp.arange(devices)
    boost = (owner_ids[None, None, :] == hottest[None, :, None]).astype(jnp.int32) * (1 << 20)
    score = (noise + favour[None, None, :] * 2048 + boost) * devices + owner_ids[None, None, :]
    unused, chosen = lax.top_k(score, wanted)
    shuffle = jax.random.randint(key_order, (devices, KVH, wanted), 0, 4096) * wanted + jnp.arange(wanted)
    order = jnp.argsort(shuffle, axis=-1)
    owners = jnp.take_along_axis(chosen, order, axis=-1).astype(jnp.int32)
    source = jnp.arange(devices, dtype=jnp.int32)[:, None, None]
    count = jnp.where(owners == source, KVB_DEV - 1, KVB_DEV)
    first_pick = jax.random.randint(key_first, (devices, KVH, wanted), 0, 1 << 16) % count
    second_pick = jax.random.randint(key_second, (devices, KVH, wanted), 0, 1 << 16) % count
    within = jnp.minimum(first_pick, second_pick)
    block = owners * KVB_DEV + within
    own_block = source * KVB_DEV + KVB_DEV - 1
    entry = jnp.where(block > own_block, block - 1, block)
    entry = entry.reshape(devices, KVH, TPD, SEL).transpose(0, 2, 1, 3).reshape(TILES, KVH, SEL)
    return entry.astype(jnp.int32)


def block_levels(stream_key, dims, cuts, least, high):
    level = 1.0
    for dim, shards_of in cuts:
        heights = jax.random.uniform(jax.random.fold_in(jax.random.fold_in(stream_key, 6), dim), (shards_of,), jnp.float32, least / len(cuts), high / len(cuts))
        level = level * jnp.repeat(jnp.exp(heights), dims[dim] // shards_of).reshape((-1,) + (1,) * (len(dims) - 1 - dim))
    return level


def normal_values(key, shape, scale, reach, cuts=(), kind=jnp.bfloat16):
    result = scale * jax.random.normal(key, shape, jnp.float32)
    if cuts:
        result = result * block_levels(key, shape, cuts, -0.22, 0.18)
    return jnp.clip(result, -reach, reach).astype(kind)


def setup_inputs(seed: int = 0) -> dict:
    splits = jax.random.split(jax.random.key(seed), 5)
    return {
        "queries": draw_queries(jax.random.fold_in(splits[4], 71), 0),
        "kv_cache": draw_kv_cache(jax.random.fold_in(splits[4], 71), 0),
        "selected": draw_selected(jax.random.fold_in(splits[4], 71), 0),
        "out_weight": normal_values(splits[3], (H * HD, DOUT), (H * HD // 2) ** -0.5, 0.1875, ((0, 4), (1, 8))),
    }


def attend(query_tile, key_rows, value_rows, visible):
    scores = jnp.einsum("igd,kd->gik", query_tile.astype(jnp.float32), key_rows.astype(jnp.float32)) * (HD ** -0.5)
    scores = jnp.where(visible[None], scores, -jnp.inf)
    row_max = jnp.max(scores, axis=2)
    weights = jnp.exp(scores - row_max[:, :, None])
    row_sum = jnp.sum(weights, axis=2)
    rounded = lax.optimization_barrier(weights.astype(jnp.bfloat16)).astype(jnp.float32)
    summed = jnp.einsum("gik,kd->gid", rounded, value_rows.astype(jnp.float32))
    return row_max, row_sum, (summed / row_sum[:, :, None]).astype(jnp.bfloat16)


def combine(row_maxes, row_sums, normeds):
    highest = row_maxes[0]
    for extra in row_maxes[1:]:
        highest = jnp.maximum(highest, extra)
    norm_sum = jnp.zeros_like(highest)
    blended = jnp.zeros(normeds[0].shape, highest.dtype)
    for top_value, sum_value, normed in zip(row_maxes, row_sums, normeds):
        factor = jnp.exp(top_value - highest) * sum_value
        norm_sum = norm_sum + factor
        blended = blended + factor[..., None] * normed.astype(highest.dtype)
    return blended / norm_sum[..., None]


def reference(queries, kv_cache, selected, out_weight):
    tiles_dev = QT_DEV // TILE
    key_offsets = jnp.arange(BLK)
    full_view = jnp.ones((TILE, BLK), dtype=bool)

    def one_tile(tile):
        device = tile // tiles_dev
        place = tile % tiles_dev
        own_block = device * KVB_DEV + KVB_DEV - 1
        query_rows = lax.dynamic_slice_in_dim(queries, (tile * TILE).astype(jnp.int32), TILE, 0)
        query_offsets = BLK - QT_DEV + place * TILE + jnp.arange(TILE)
        causal = key_offsets[None, :] <= query_offsets[:, None]
        results = []
        for head in range(KVH):
            query_tile = query_rows[:, head * GROUP * HD:(head + 1) * GROUP * HD].reshape(TILE, GROUP, HD)
            chosen = [own_block]
            for pick in range(SEL):
                entry = selected[tile, head, pick]
                chosen.append(jnp.where(entry >= own_block, entry + 1, entry))
            maxima, sums, outs = [], [], []
            for index, block in enumerate(chosen):
                start = (block * BLK).astype(jnp.int32)
                pair = lax.dynamic_slice(kv_cache, (jnp.int32(0), start, jnp.int32(head * HD)), (2, BLK, HD))
                visible = causal if index == 0 else full_view
                top_value, sum_value, normed = attend(query_tile, pair[0], pair[1], visible)
                maxima.append(top_value)
                sums.append(sum_value)
                outs.append(normed)
            mixed = combine(maxima, sums, outs)
            results.append(jnp.transpose(mixed, (1, 0, 2)).reshape(TILE, GROUP * HD))
        return jnp.concatenate(results, axis=1).astype(jnp.bfloat16)

    attention = lax.map(one_tile, jnp.arange(TILES, dtype=jnp.int32)).reshape(QTOK, H * HD)
    total = jnp.zeros((QTOK, DOUT), jnp.float32)
    for head in range(KVH):
        lower = head * GROUP * HD
        upper = (head + 1) * GROUP * HD
        term = jnp.dot(attention[:, lower:upper], out_weight[lower:upper], preferred_element_type=jnp.float32)
        total = total + lax.optimization_barrier(term.astype(jnp.bfloat16)).astype(jnp.float32)
    return total.astype(jnp.bfloat16)
```

```python
import functools
import math

import jax
import jax.numpy as jnp
from jax import lax
from jax.experimental import pallas as pl
from jax.experimental.pallas import tpu as pltpu
from jax.sharding import PartitionSpec as P

GROUP = 4
HD = 128
BLK = 1024
TILE = 128
SEL = 2
ROWS = GROUP * TILE
SLOT = ROWS + 16
SCALE = HD ** (-0.5)
LOG2E = math.log2(math.e)
VMEM_LIMIT = 48 * 1024 * 1024

vmem = pl.BlockSpec(memory_space=pltpu.VMEM)
smem = pl.BlockSpec(memory_space=pltpu.SMEM)
hbm = pl.BlockSpec(memory_space=pl.ANY)


def params():
    return pltpu.CompilerParams(vmem_limit_bytes=VMEM_LIMIT)


def route(selected_ref, own_seq, peer, tiles, blocks):
    own_block = own_seq * blocks + blocks - 1
    tile, block, filled = jnp.int32(0), jnp.int32(0), jnp.int32(0)
    for request in range(tiles * SEL):
        chosen = selected_ref[request]
        target = jnp.where(chosen >= own_block, chosen + 1, chosen)
        here = lax.div(target, jnp.int32(blocks)) == peer
        tile = jnp.where(here, request // SEL, tile)
        block = jnp.where(here, lax.rem(target, jnp.int32(blocks)), block)
        filled = jnp.where(here, 1, filled)
    return tile, block, filled


def pack_kernel(tiles, blocks, me_ref, selected_ref, query_ref, *slots):
    for offset, slot in enumerate(slots):
        peer = me_ref[0] ^ offset
        tile, block, _ = route(selected_ref, me_ref[0], peer, tiles, blocks)
        rows = pl.ds(pl.multiple_of(tile * TILE, TILE), TILE)
        for head in range(GROUP):
            slot[head * TILE : (head + 1) * TILE, :] = query_ref[rows, head * HD : (head + 1) * HD]
        slot[ROWS:SLOT, :] = jnp.full((16, HD), block.astype(jnp.float32)).astype(jnp.bfloat16)


def pack(me, selected, queries, seq_count, blocks):
    tiles = queries.shape[0] // TILE
    return pl.pallas_call(
        functools.partial(pack_kernel, tiles, blocks),
        out_shape=[jax.ShapeDtypeStruct((SLOT, HD), jnp.bfloat16)] * seq_count,
        in_specs=[smem, smem, vmem],
        out_specs=[vmem] * seq_count,
        compiler_params=params(),
        name="pack_queries",
    )(me, selected, queries)


def attend(query, keys, values, first_offset, out_ref):
    scores = lax.dot_general(
        query, keys, (((1,), (1,)), ((), ())), preferred_element_type=jnp.float32
    )
    if first_offset is not None:
        offsets = first_offset + lax.rem(
            lax.broadcasted_iota(jnp.int32, (ROWS, BLK), 0), jnp.int32(TILE)
        )
        seen = lax.broadcasted_iota(jnp.int32, (ROWS, BLK), 1) <= offsets
        scores = jnp.where(seen, scores, -jnp.inf)
    top = jnp.max(scores, axis=1, keepdims=True)
    weights = jnp.exp2((scores - top) * (SCALE * LOG2E))
    total = jnp.sum(weights, axis=1, keepdims=True)
    summed = jnp.dot(weights.astype(jnp.bfloat16), values, preferred_element_type=jnp.float32)
    out_ref[0:ROWS, :] = (summed / total).astype(jnp.bfloat16)
    level = top * SCALE + jnp.log(total)
    lane = lax.rem(lax.broadcasted_iota(jnp.int32, (TILE, TILE), 1), jnp.int32(GROUP))
    spread = jnp.zeros((TILE, TILE), jnp.float32)
    for head in range(GROUP):
        spread = jnp.where(lane == head, level[head * TILE : (head + 1) * TILE], spread)
    lines = spread.T[0:16]
    high = lines.astype(jnp.bfloat16).astype(jnp.float32)
    middle = (lines - high).astype(jnp.bfloat16).astype(jnp.float32)
    low = lines - high - middle
    row = lax.broadcasted_iota(jnp.int32, (16, TILE), 0)
    parts = jnp.where(row < GROUP, high, jnp.where(row < 2 * GROUP, middle, low))
    out_ref[ROWS:SLOT, :] = parts.astype(jnp.bfloat16)


def own_kernel(tiles, blocks, query_ref, kv_ref, out_ref, keys, values, sems):
    start = (blocks - 1) * BLK
    copies = [
        pltpu.make_async_copy(kv_ref.at[0, pl.ds(start, BLK)], keys, sems.at[0]),
        pltpu.make_async_copy(kv_ref.at[1, pl.ds(start, BLK)], values, sems.at[1]),
    ]
    for copy in copies:
        copy.start()
    for copy in copies:
        copy.wait()

    def one(tile, carry):
        rows = pl.ds(pl.multiple_of(tile * TILE, TILE), TILE)
        query = jnp.concatenate(
            [query_ref[rows, head * HD : (head + 1) * HD] for head in range(GROUP)], axis=0
        )
        first_offset = BLK - tiles * TILE + tile * TILE
        attend(query, keys[...], values[...], first_offset, out_ref.at[tile])
        return carry

    lax.fori_loop(0, tiles, one, 0)


def own_pieces(queries, kv_cache):
    tiles, blocks = queries.shape[0] // TILE, kv_cache.shape[1] // BLK
    return pl.pallas_call(
        functools.partial(own_kernel, tiles, blocks),
        out_shape=jax.ShapeDtypeStruct((tiles, SLOT, HD), jnp.bfloat16),
        in_specs=[vmem, hbm],
        out_specs=vmem,
        scratch_shapes=[
            pltpu.VMEM((BLK, HD), jnp.bfloat16),
            pltpu.VMEM((BLK, HD), jnp.bfloat16),
            pltpu.SemaphoreType.DMA((2,)),
        ],
        compiler_params=params(),
        cost_estimate=pl.CostEstimate(
            flops=4 * tiles * ROWS * BLK * HD, bytes_accessed=4 * BLK * HD, transcendentals=tiles * ROWS * BLK
        ),
        name="own_pieces",
    )(queries, kv_cache)


def serve_kernel(slot_ref, kv_ref, out_ref, keys, values, sems):
    number = jnp.max(slot_ref[ROWS:SLOT, :].astype(jnp.float32)).astype(jnp.int32)
    start = pl.multiple_of(number * BLK, BLK)
    key_copy = pltpu.make_async_copy(kv_ref.at[0, pl.ds(start, BLK)], keys, sems.at[0])
    value_copy = pltpu.make_async_copy(kv_ref.at[1, pl.ds(start, BLK)], values, sems.at[1])
    key_copy.start()
    value_copy.start()
    key_copy.wait()
    value_copy.wait()
    attend(slot_ref[0:ROWS, :], keys[...], values[...], None, out_ref)


def serve(slot, kv_cache):
    return pl.pallas_call(
        serve_kernel,
        out_shape=jax.ShapeDtypeStruct((SLOT, HD), jnp.bfloat16),
        in_specs=[vmem, hbm],
        out_specs=vmem,
        scratch_shapes=[
            pltpu.VMEM((BLK, HD), jnp.bfloat16),
            pltpu.VMEM((BLK, HD), jnp.bfloat16),
            pltpu.SemaphoreType.DMA((2,)),
        ],
        compiler_params=params(),
        cost_estimate=pl.CostEstimate(
            flops=4 * ROWS * BLK * HD, bytes_accessed=4 * BLK * HD, transcendentals=ROWS * BLK
        ),
        name="serve_slot",
    )(slot, kv_cache)


def levels_of(parts):
    parts = parts.astype(jnp.float32)
    return parts[0:GROUP] + parts[GROUP : 2 * GROUP] + parts[2 * GROUP : 3 * GROUP]


def combine_kernel(tiles, blocks, seq_count, me_ref, selected_ref, own_ref, *refs):
    slots, out_ref, blend = refs[:seq_count], refs[seq_count], refs[seq_count + 1]
    routes = [
        route(selected_ref, me_ref[0], me_ref[0] ^ offset, tiles, blocks)
        for offset in range(seq_count)
    ]
    slot_levels = [levels_of(slot[ROWS:SLOT, :]) for slot in slots]
    for tile in range(tiles):
        own_level = levels_of(own_ref[tile, ROWS:SLOT, :])
        mine = [(filled > 0) & (number == tile) for number, _, filled in routes]
        levels = [own_level] + [
            jnp.where(used, level, -jnp.inf) for used, level in zip(mine, slot_levels)
        ]
        highest = functools.reduce(jnp.maximum, levels)
        factors = [jnp.exp(level - highest) for level in levels]
        norm = functools.reduce(jnp.add, factors)
        lines = jnp.concatenate([factor / norm for factor in factors], axis=0)
        count = lines.shape[0]
        room = -count % TILE
        if room:
            lines = jnp.concatenate([lines, jnp.zeros((room, TILE), jnp.float32)], axis=0)
        columns = jnp.concatenate(
            [lines[part * TILE : (part + 1) * TILE].T for part in range(lines.shape[0] // TILE)],
            axis=1,
        )
        for head in range(GROUP):
            part = slice(head * TILE, (head + 1) * TILE)
            blend[part, :] = columns[:, head : head + 1] * own_ref[tile, part, :].astype(jnp.float32)
        for index, used in enumerate(mine):

            @pl.when(used)
            def _(index=index, columns=columns):
                for head in range(GROUP):
                    part = slice(head * TILE, (head + 1) * TILE)
                    column = (index + 1) * GROUP + head
                    blend[part, :] += columns[:, column : column + 1] * slots[index][part, :].astype(
                        jnp.float32
                    )

        for head in range(GROUP):
            out_ref[tile * TILE : (tile + 1) * TILE, head * HD : (head + 1) * HD] = blend[
                head * TILE : (head + 1) * TILE, :
            ].astype(jnp.bfloat16)


def combine(me, selected, own, slots, blocks):
    tiles = own.shape[0]
    seq_count = len(slots)
    return pl.pallas_call(
        functools.partial(combine_kernel, tiles, blocks, seq_count),
        out_shape=jax.ShapeDtypeStruct((tiles * TILE, GROUP * HD), jnp.bfloat16),
        in_specs=[smem, smem, vmem] + [vmem] * seq_count,
        out_specs=vmem,
        scratch_shapes=[pltpu.VMEM((ROWS, HD), jnp.float32)],
        compiler_params=params(),
        name="combine_pieces",
    )(me, selected, own, *slots)


def project_kernel(heads, me_ref, *refs):
    attentions, shards, out_ref = refs[:heads], refs[heads:-1], refs[-1]
    width = shards[0].shape[1]
    order = len(shards) // heads
    z, x, h = me_ref[0], me_ref[1], me_ref[2]
    for side in range(order):
        total = None
        for index in range(heads):
            place = (z ^ index) ^ h
            left = attentions[0][...]
            for other in range(1, heads):
                left = jnp.where(place == other, attentions[other][...], left)
            term = jnp.dot(left, shards[side * heads + index][...], preferred_element_type=jnp.float32)
            total = term if total is None else total + term
        start = pl.multiple_of((x ^ side) * width, width)
        out_ref[:, pl.ds(start, width)] = total.astype(jnp.bfloat16)


def project(numbers, attentions, shards):
    rows, width = attentions[0].shape[0], shards[0].shape[1]
    heads = len(attentions)
    columns = width * len(shards) // heads
    return pl.pallas_call(
        functools.partial(project_kernel, heads),
        out_shape=jax.ShapeDtypeStruct((rows, columns), jnp.bfloat16),
        in_specs=[smem] + [vmem] * (heads + len(shards)),
        out_specs=vmem,
        compiler_params=params(),
        name="project",
    )(numbers, *attentions, *shards)


def pairs(count, offset):
    return [(index, index ^ offset) for index in range(count)]


def spread_weight(weight, kvh_count):
    joint = ("seq", "kvh")

    def jump(flip):
        moves = []
        for z in range(kvh_count):
            for x in range(2):
                for h in range(kvh_count):
                    moves.append(((z * 2 + x) * kvh_count + h, ((h ^ flip) * 2 + x) * kvh_count + z))
        return lax.ppermute(weight, joint, moves)

    seq_count = 2 * kvh_count
    shards = [None] * kvh_count
    for index in range(0, kvh_count, 2):
        shards[index] = jump(index)
        shards[index + 1] = lax.ppermute(shards[index], "seq", pairs(seq_count, 2))
    return shards + [lax.ppermute(shard, "seq", pairs(seq_count, 1)) for shard in shards]


def per_device(queries, kv_cache, selected, out_weight):
    seq_count, kvh_count = lax.axis_size("seq"), lax.axis_size("kvh")
    seq, kvh = lax.axis_index("seq"), lax.axis_index("kvh")
    blocks = kv_cache.shape[1] // BLK
    me = seq.astype(jnp.int32).reshape(1)
    requests = selected.reshape(-1)
    outgoing = pack(me, requests, queries, seq_count, blocks)
    arrived = [outgoing[0]] + [
        lax.ppermute(outgoing[offset], "seq", pairs(seq_count, offset))
        for offset in range(1, seq_count)
    ]
    own = own_pieces(queries, kv_cache)
    returned = [
        serve(arrived[0], kv_cache)
    ] + [
        lax.ppermute(serve(arrived[offset], kv_cache), "seq", pairs(seq_count, offset))
        for offset in range(1, seq_count)
    ]
    attention = combine(me, requests, own, returned, blocks)
    if seq_count == 2 * kvh_count and kvh_count & (kvh_count - 1) == 0:
        shards = spread_weight(out_weight, kvh_count)
        gathered = [attention]
        bit = kvh_count // 2
        parts = {0: attention}
        while bit:
            for offset in list(parts):
                parts[offset | bit] = lax.ppermute(parts[offset], "kvh", pairs(kvh_count, bit))
            bit //= 2
        gathered = [parts[offset] for offset in range(kvh_count)]
        numbers = jnp.stack([seq // 2, seq % 2, kvh]).astype(jnp.int32)
        return project(numbers, gathered, shards)
    column_terms = jnp.dot(
        attention,
        lax.all_gather(out_weight, "seq", axis=1, tiled=True),
        preferred_element_type=jnp.float32,
    )
    return lax.psum_scatter(
        column_terms.astype(jnp.bfloat16), "kvh", scatter_dimension=1, tiled=True
    )


def solution(mesh):
    in_specs = (P("seq", "kvh"), P(None, "seq", "kvh"), P("seq", "kvh", None), P("kvh", "seq"))
    out_specs = P("seq", "kvh")
    return jax.shard_map(
        per_device, mesh=mesh, in_specs=in_specs, out_specs=out_specs, check_vma=False
    )
```

```python
import functools
import math

import jax
import jax.numpy as jnp
from jax import lax
from jax.experimental import pallas as pl
from jax.experimental.pallas import tpu as pltpu
from jax.sharding import PartitionSpec as P

GROUP = 4
HD = 128
BLK = 1024
TILE = 128
SEL = 2
ROWS = GROUP * TILE
SLOT = ROWS + 16
SCALE = HD ** (-0.5)
LOG2E = math.log2(math.e)
VMEM_LIMIT = 48 * 1024 * 1024

vmem = pl.BlockSpec(memory_space=pltpu.VMEM)
smem = pl.BlockSpec(memory_space=pltpu.SMEM)
hbm = pl.BlockSpec(memory_space=pltpu.HBM)
anywhere = pl.BlockSpec(memory_space=pl.ANY)


def params():
    return pltpu.CompilerParams(vmem_limit_bytes=VMEM_LIMIT)


def route(selected_ref, own_seq, peer, tiles, blocks):
    own_block = own_seq * blocks + blocks - 1
    tile, block, filled = jnp.int32(0), jnp.int32(0), jnp.int32(0)
    for request in range(tiles * SEL):
        chosen = selected_ref[request // SEL, 0, request % SEL]
        target = jnp.where(chosen >= own_block, chosen + 1, chosen)
        here = lax.div(target, jnp.int32(blocks)) == peer
        tile = jnp.where(here, request // SEL, tile)
        block = jnp.where(here, lax.rem(target, jnp.int32(blocks)), block)
        filled = jnp.where(here, 1, filled)
    return tile, block, filled


def pack_kernel(tiles, blocks, me_ref, selected_ref, query_ref, *slots):
    for offset, slot in enumerate(slots):
        peer = me_ref[0] ^ offset
        tile, block, _ = route(selected_ref, me_ref[0], peer, tiles, blocks)
        rows = pl.ds(pl.multiple_of(tile * TILE, TILE), TILE)
        for head in range(GROUP):
            slot[head * TILE : (head + 1) * TILE, :] = query_ref[rows, head * HD : (head + 1) * HD]
        slot[ROWS:SLOT, :] = jnp.full((16, HD), block.astype(jnp.float32)).astype(jnp.bfloat16)


def pack(me, selected, queries, seq_count, blocks):
    tiles = queries.shape[0] // TILE
    return pl.pallas_call(
        functools.partial(pack_kernel, tiles, blocks),
        out_shape=[jax.ShapeDtypeStruct((SLOT, HD), jnp.bfloat16)] * seq_count,
        in_specs=[smem, smem, vmem],
        out_specs=[vmem] * seq_count,
        compiler_params=params(),
        name="pack_queries",
    )(me, selected, queries)


def attend(query, keys, values, first_offset, out_ref):
    scores = lax.dot_general(
        query, keys, (((1,), (1,)), ((), ())), preferred_element_type=jnp.float32
    )
    if first_offset is not None:
        offsets = first_offset + lax.rem(
            lax.broadcasted_iota(jnp.int32, (ROWS, BLK), 0), jnp.int32(TILE)
        )
        seen = lax.broadcasted_iota(jnp.int32, (ROWS, BLK), 1) <= offsets
        scores = jnp.where(seen, scores, -jnp.inf)
    top = jnp.max(scores, axis=1, keepdims=True)
    weights = jnp.exp2((scores - top) * (SCALE * LOG2E))
    total = jnp.sum(weights, axis=1, keepdims=True)
    summed = jnp.dot(weights.astype(jnp.bfloat16), values, preferred_element_type=jnp.float32)
    out_ref[0:ROWS, :] = (summed / total).astype(jnp.bfloat16)
    level = top * SCALE + jnp.log(total)
    lane = lax.rem(lax.broadcasted_iota(jnp.int32, (TILE, TILE), 1), jnp.int32(GROUP))
    spread = jnp.zeros((TILE, TILE), jnp.float32)
    for head in range(GROUP):
        spread = jnp.where(lane == head, level[head * TILE : (head + 1) * TILE], spread)
    lines = spread.T[0:16]
    high = lines.astype(jnp.bfloat16).astype(jnp.float32)
    middle = (lines - high).astype(jnp.bfloat16).astype(jnp.float32)
    low = lines - high - middle
    row = lax.broadcasted_iota(jnp.int32, (16, TILE), 0)
    parts = jnp.where(row < GROUP, high, jnp.where(row < 2 * GROUP, middle, low))
    out_ref[ROWS:SLOT, :] = parts.astype(jnp.bfloat16)


def own_kernel(tiles, blocks, query_ref, kv_ref, *refs):
    out_ref, keys, values, sems = refs[-4:]
    start = (blocks - 1) * BLK
    copies = [
        pltpu.make_async_copy(kv_ref.at[0, pl.ds(start, BLK)], keys, sems.at[0]),
        pltpu.make_async_copy(kv_ref.at[1, pl.ds(start, BLK)], values, sems.at[1]),
    ]
    for copy in copies:
        copy.start()
    for copy in copies:
        copy.wait()

    def one(tile, carry):
        rows = pl.ds(pl.multiple_of(tile * TILE, TILE), TILE)
        query = jnp.concatenate(
            [query_ref[rows, head * HD : (head + 1) * HD] for head in range(GROUP)], axis=0
        )
        first_offset = BLK - tiles * TILE + tile * TILE
        attend(query, keys[...], values[...], first_offset, out_ref.at[tile])
        return carry

    lax.fori_loop(0, tiles, one, 0)


def own_pieces(queries, kv_cache, after):
    tiles, blocks = queries.shape[0] // TILE, kv_cache.shape[1] // BLK
    return pl.pallas_call(
        functools.partial(own_kernel, tiles, blocks),
        out_shape=jax.ShapeDtypeStruct((tiles, SLOT, HD), jnp.bfloat16),
        in_specs=[vmem, hbm] + [anywhere] * len(after),
        out_specs=vmem,
        scratch_shapes=[
            pltpu.VMEM((BLK, HD), jnp.bfloat16),
            pltpu.VMEM((BLK, HD), jnp.bfloat16),
            pltpu.SemaphoreType.DMA((2,)),
        ],
        compiler_params=params(),
        cost_estimate=pl.CostEstimate(flops=1 << 36, bytes_accessed=1 << 30, transcendentals=1),
        name="own_pieces",
    )(queries, kv_cache, *after)


def serve_kernel(count, *refs):
    slots, kv_ref, outs = refs[:count], refs[count], refs[-count - 3 : -3]
    keys, values, sems = refs[-3:]
    copies = []
    for index, slot in enumerate(slots):
        number = jnp.max(slot[ROWS:SLOT, :].astype(jnp.float32)).astype(jnp.int32)
        start = pl.multiple_of(number * BLK, BLK)
        for half, buffer in enumerate((keys, values)):
            copy = pltpu.make_async_copy(
                kv_ref.at[half, pl.ds(start, BLK)], buffer.at[index], sems.at[half, index]
            )
            copy.start()
            copies.append(copy)
    for index, slot in enumerate(slots):
        copies[2 * index].wait()
        copies[2 * index + 1].wait()
        attend(slot[0:ROWS, :], keys[index], values[index], None, outs[index])


def serve(slots, kv_cache, after):
    count = len(slots)
    return pl.pallas_call(
        functools.partial(serve_kernel, count),
        out_shape=[jax.ShapeDtypeStruct((SLOT, HD), jnp.bfloat16)] * count,
        in_specs=[vmem] * count + [hbm] + [anywhere] * len(after),
        out_specs=[vmem] * count,
        scratch_shapes=[
            pltpu.VMEM((count, BLK, HD), jnp.bfloat16),
            pltpu.VMEM((count, BLK, HD), jnp.bfloat16),
            pltpu.SemaphoreType.DMA((2, count)),
        ],
        compiler_params=params(),
        cost_estimate=pl.CostEstimate(flops=1 << 36, bytes_accessed=1 << 30, transcendentals=1),
        name="serve_slots",
    )(*slots, kv_cache, *after)


def levels_of(parts):
    parts = parts.astype(jnp.float32)
    return parts[0:GROUP] + parts[GROUP : 2 * GROUP] + parts[2 * GROUP : 3 * GROUP]


def combine_kernel(tiles, blocks, seq_count, me_ref, selected_ref, own_ref, *refs):
    slots, out_ref, blend = refs[:seq_count], refs[-2], refs[-1]
    routes = [
        route(selected_ref, me_ref[0], me_ref[0] ^ offset, tiles, blocks)
        for offset in range(seq_count)
    ]
    slot_levels = [levels_of(slot[ROWS:SLOT, :]) for slot in slots]
    for tile in range(tiles):
        own_level = levels_of(own_ref[tile, ROWS:SLOT, :])
        mine = [(filled > 0) & (number == tile) for number, _, filled in routes]
        levels = [own_level] + [
            jnp.where(used, level, -jnp.inf) for used, level in zip(mine, slot_levels)
        ]
        highest = functools.reduce(jnp.maximum, levels)
        factors = [jnp.exp(level - highest) for level in levels]
        norm = functools.reduce(jnp.add, factors)
        lines = jnp.concatenate([factor / norm for factor in factors], axis=0)
        count = lines.shape[0]
        room = -count % TILE
        if room:
            lines = jnp.concatenate([lines, jnp.zeros((room, TILE), jnp.float32)], axis=0)
        columns = jnp.concatenate(
            [lines[part * TILE : (part + 1) * TILE].T for part in range(lines.shape[0] // TILE)],
            axis=1,
        )
        for head in range(GROUP):
            part = slice(head * TILE, (head + 1) * TILE)
            blend[part, :] = columns[:, head : head + 1] * own_ref[tile, part, :].astype(jnp.float32)
        for index, used in enumerate(mine):

            @pl.when(used)
            def _(index=index, columns=columns):
                for head in range(GROUP):
                    part = slice(head * TILE, (head + 1) * TILE)
                    column = (index + 1) * GROUP + head
                    blend[part, :] += columns[:, column : column + 1] * slots[index][part, :].astype(
                        jnp.float32
                    )

        for head in range(GROUP):
            out_ref[tile * TILE : (tile + 1) * TILE, head * HD : (head + 1) * HD] = blend[
                head * TILE : (head + 1) * TILE, :
            ].astype(jnp.bfloat16)


def combine(me, selected, own, slots, blocks, after):
    tiles = own.shape[0]
    seq_count = len(slots)
    return pl.pallas_call(
        functools.partial(combine_kernel, tiles, blocks, seq_count),
        out_shape=jax.ShapeDtypeStruct((tiles * TILE, GROUP * HD), jnp.bfloat16),
        in_specs=[smem, smem, vmem] + [vmem] * seq_count + [anywhere] * len(after),
        out_specs=vmem,
        scratch_shapes=[pltpu.VMEM((ROWS, HD), jnp.float32)],
        compiler_params=params(),
        name="combine_pieces",
    )(me, selected, own, *slots, *after)


def project_kernel(heads, me_ref, *refs):
    attentions, stacks, out_ref = refs[:heads], refs[heads:-1], refs[-1]
    depth, width = attentions[0].shape[1], stacks[0].shape[1]
    z, x, h = me_ref[0], me_ref[1], me_ref[2]
    lefts = []
    for index in range(heads):
        place = (z ^ index) ^ h
        left = attentions[0][...]
        for other in range(1, heads):
            left = jnp.where(place == other, attentions[other][...], left)
        lefts.append(left)
    for side in range(2):
        total = None
        for index in range(heads):
            stack = stacks[2 * side + (index & 1)]
            part = slice((index >> 1) * depth, ((index >> 1) + 1) * depth)
            term = jnp.dot(lefts[index], stack[part, :], preferred_element_type=jnp.float32)
            total = term if total is None else total + term
        start = pl.multiple_of((x ^ side) * width, width)
        out_ref[:, pl.ds(start, width)] = total.astype(jnp.bfloat16)


def project(numbers, attentions, stacks):
    rows, width = attentions[0].shape[0], stacks[0].shape[1]
    heads = len(attentions)
    return pl.pallas_call(
        functools.partial(project_kernel, heads),
        out_shape=jax.ShapeDtypeStruct((rows, 2 * width), jnp.bfloat16),
        in_specs=[smem] + [vmem] * (heads + len(stacks)),
        out_specs=vmem,
        compiler_params=params(),
        name="project",
    )(numbers, *attentions, *stacks)


def pairs(count, offset):
    return [(index, index ^ offset) for index in range(count)]


def jump(weight, kvh_count, flip):
    moves = []
    for z in range(kvh_count):
        for x in range(2):
            for h in range(kvh_count):
                moves.append(((z * 2 + x) * kvh_count + h, ((h ^ flip) * 2 + x) * kvh_count + z))
    return lax.ppermute(weight, ("seq", "kvh"), moves)


def per_device(queries, kv_cache, selected, out_weight):
    seq_count, kvh_count = lax.axis_size("seq"), lax.axis_size("kvh")
    seq, kvh = lax.axis_index("seq"), lax.axis_index("kvh")
    blocks = kv_cache.shape[1] // BLK
    me = seq.astype(jnp.int32).reshape(1)
    requests = selected
    fast = seq_count == 2 * kvh_count and kvh_count == 4

    def move(array, offset):
        return lax.ppermute(array, "seq", pairs(seq_count, offset))

    stack = stack_z = stack_x = stack_zx = None
    if fast:
        jumps = [jump(out_weight, kvh_count, 0), jump(out_weight, kvh_count, 2)]
        stack = jnp.concatenate(jumps, axis=0)
        stack_z = move(stack, 2)
        stack_x = move(stack, 1)
        stack_zx = move(stack_z, 1)
    outgoing = pack(me, requests, queries, seq_count, blocks)
    arrived = {offset: move(outgoing[offset], offset) for offset in range(1, seq_count)}
    returned = {}

    def answer(offsets, after):
        answers = serve([arrived[offset] for offset in offsets], kv_cache, [a for a in after if a is not None])
        for offset, result in zip(offsets, answers):
            returned[offset] = move(result, offset)
        return answers[-1]

    own = own_pieces(queries, kv_cache, [outgoing[0]])
    last = returned[0] = serve([outgoing[0]], kv_cache, [own])[0]
    last = answer([1, 2, 3], [last, stack])
    last = answer([4, 5], [last])
    for place in range(6, seq_count, 2):
        last = answer([place, place + 1], [last, stack_x])
    returned = [returned[offset] for offset in range(seq_count)]
    attention = combine(me, requests, own, returned, blocks, [stack_z] if fast else [])
    if fast:
        other_y = lax.ppermute(attention, "kvh", pairs(kvh_count, 2))
        other_core = lax.ppermute(attention, "kvh", pairs(kvh_count, 1))
        both = lax.ppermute(other_y, "kvh", pairs(kvh_count, 1))
        gathered = [attention, other_core, other_y, both]
        stacks = [stack, stack_z, stack_x, stack_zx]
        numbers = jnp.stack([lax.shift_right_logical(seq, 1), seq & 1, kvh]).astype(jnp.int32)
        return project(numbers, gathered, stacks)
    column_terms = jnp.dot(
        attention,
        lax.all_gather(out_weight, "seq", axis=1, tiled=True),
        preferred_element_type=jnp.float32,
    )
    return lax.psum_scatter(
        column_terms.astype(jnp.bfloat16), "kvh", scatter_dimension=1, tiled=True
    )


def solution(mesh):
    in_specs = (P("seq", "kvh"), P(None, "seq", "kvh"), P("seq", "kvh", None), P("kvh", "seq"))
    out_specs = P("seq", "kvh")
    return jax.shard_map(
        per_device, mesh=mesh, in_specs=in_specs, out_specs=out_specs, check_vma=False
    )
```

```python
import functools
import math

import jax
import jax.numpy as jnp
from jax import lax
from jax.experimental import pallas as pl
from jax.experimental.pallas import tpu as pltpu
from jax.sharding import PartitionSpec as P

GROUP = 4
HD = 128
BLK = 1024
TILE = 128
SEL = 2
ROWS = GROUP * TILE
SLOT = ROWS + 16
NEAR = 4
SCALE = HD ** (-0.5)
LOG2E = math.log2(math.e)
VMEM_LIMIT = 48 * 1024 * 1024

vmem = pl.BlockSpec(memory_space=pltpu.VMEM)
smem = pl.BlockSpec(memory_space=pltpu.SMEM)
hbm = pl.BlockSpec(memory_space=pltpu.HBM)
anywhere = pl.BlockSpec(memory_space=pl.ANY)


def params():
    return pltpu.CompilerParams(vmem_limit_bytes=VMEM_LIMIT)


def route(selected_ref, own_seq, peer, tiles, blocks):
    own_block = own_seq * blocks + blocks - 1
    tile, block, filled = jnp.int32(0), jnp.int32(0), jnp.int32(0)
    for request in range(tiles * SEL):
        chosen = selected_ref[request // SEL, 0, request % SEL]
        target = jnp.where(chosen >= own_block, chosen + 1, chosen)
        here = lax.div(target, jnp.int32(blocks)) == peer
        tile = jnp.where(here, request // SEL, tile)
        block = jnp.where(here, lax.rem(target, jnp.int32(blocks)), block)
        filled = jnp.where(here, 1, filled)
    return tile, block, filled


def pack_kernel(tiles, blocks, me_ref, selected_ref, query_ref, near_ref, *far_refs):
    def fill(slot, peer):
        tile, block, _ = route(selected_ref, me_ref[0], peer, tiles, blocks)
        rows = pl.ds(pl.multiple_of(tile * TILE, TILE), TILE)
        for head in range(GROUP):
            slot[head * TILE : (head + 1) * TILE, :] = query_ref[rows, head * HD : (head + 1) * HD]
        slot[ROWS:SLOT, :] = jnp.full((16, HD), block.astype(jnp.float32)).astype(jnp.bfloat16)

    for place in range(NEAR):
        fill(near_ref.at[place], (me_ref[0] & ~(NEAR - 1)) + place)
    for index, slot in enumerate(far_refs):
        fill(slot, me_ref[0] ^ (NEAR + index))


def pack(me, selected, queries, seq_count, blocks):
    tiles = queries.shape[0] // TILE
    return pl.pallas_call(
        functools.partial(pack_kernel, tiles, blocks),
        out_shape=[jax.ShapeDtypeStruct((NEAR, SLOT, HD), jnp.bfloat16)]
        + [jax.ShapeDtypeStruct((SLOT, HD), jnp.bfloat16)] * (seq_count - NEAR),
        in_specs=[smem, smem, vmem],
        out_specs=[vmem] * (seq_count - NEAR + 1),
        compiler_params=params(),
        name="pack_queries",
    )(me, selected, queries)


def attend(query, keys, values, first_offset, out_ref):
    scores = lax.dot_general(
        query, keys, (((1,), (1,)), ((), ())), preferred_element_type=jnp.float32
    )
    if first_offset is not None:
        offsets = first_offset + lax.rem(
            lax.broadcasted_iota(jnp.int32, (ROWS, BLK), 0), jnp.int32(TILE)
        )
        seen = lax.broadcasted_iota(jnp.int32, (ROWS, BLK), 1) <= offsets
        scores = jnp.where(seen, scores, -jnp.inf)
    top = jnp.max(scores, axis=1, keepdims=True)
    weights = jnp.exp2((scores - top) * (SCALE * LOG2E))
    total = jnp.sum(weights, axis=1, keepdims=True)
    summed = jnp.dot(weights.astype(jnp.bfloat16), values, preferred_element_type=jnp.float32)
    out_ref[0:ROWS, :] = (summed / total).astype(jnp.bfloat16)
    level = top * SCALE + jnp.log(total)
    lane = lax.rem(lax.broadcasted_iota(jnp.int32, (TILE, TILE), 1), jnp.int32(GROUP))
    spread = jnp.zeros((TILE, TILE), jnp.float32)
    for head in range(GROUP):
        spread = jnp.where(lane == head, level[head * TILE : (head + 1) * TILE], spread)
    lines = spread.T[0:16]
    high = lines.astype(jnp.bfloat16).astype(jnp.float32)
    middle = (lines - high).astype(jnp.bfloat16).astype(jnp.float32)
    low = lines - high - middle
    row = lax.broadcasted_iota(jnp.int32, (16, TILE), 0)
    parts = jnp.where(row < GROUP, high, jnp.where(row < 2 * GROUP, middle, low))
    out_ref[ROWS:SLOT, :] = parts.astype(jnp.bfloat16)


def own_kernel(tiles, blocks, query_ref, kv_ref, *refs):
    out_ref, keys, values, sems = refs[-4:]
    start = (blocks - 1) * BLK
    copies = [
        pltpu.make_async_copy(kv_ref.at[0, pl.ds(start, BLK)], keys, sems.at[0]),
        pltpu.make_async_copy(kv_ref.at[1, pl.ds(start, BLK)], values, sems.at[1]),
    ]
    for copy in copies:
        copy.start()
    for copy in copies:
        copy.wait()

    def one(tile, carry):
        rows = pl.ds(pl.multiple_of(tile * TILE, TILE), TILE)
        query = jnp.concatenate(
            [query_ref[rows, head * HD : (head + 1) * HD] for head in range(GROUP)], axis=0
        )
        first_offset = BLK - tiles * TILE + tile * TILE
        attend(query, keys[...], values[...], first_offset, out_ref.at[tile])
        return carry

    lax.fori_loop(0, tiles, one, 0)


def own_pieces(queries, kv_cache, after):
    tiles, blocks = queries.shape[0] // TILE, kv_cache.shape[1] // BLK
    return pl.pallas_call(
        functools.partial(own_kernel, tiles, blocks),
        out_shape=jax.ShapeDtypeStruct((tiles, SLOT, HD), jnp.bfloat16),
        in_specs=[vmem, hbm] + [anywhere] * len(after),
        out_specs=vmem,
        scratch_shapes=[
            pltpu.VMEM((BLK, HD), jnp.bfloat16),
            pltpu.VMEM((BLK, HD), jnp.bfloat16),
            pltpu.SemaphoreType.DMA((2,)),
        ],
        compiler_params=params(),
        cost_estimate=pl.CostEstimate(flops=1 << 36, bytes_accessed=1 << 30, transcendentals=1),
        name="own_pieces",
    )(queries, kv_cache, *after)


def serve_kernel(count, *refs):
    slots, kv_ref, outs = refs[:count], refs[count], refs[-count - 3 : -3]
    keys, values, sems = refs[-3:]
    copies = []
    for index, slot in enumerate(slots):
        number = jnp.max(slot[ROWS:SLOT, :].astype(jnp.float32)).astype(jnp.int32)
        start = pl.multiple_of(number * BLK, BLK)
        for half, buffer in enumerate((keys, values)):
            copy = pltpu.make_async_copy(
                kv_ref.at[half, pl.ds(start, BLK)], buffer.at[index], sems.at[half, index]
            )
            copy.start()
            copies.append(copy)
    for index, slot in enumerate(slots):
        copies[2 * index].wait()
        copies[2 * index + 1].wait()
        attend(slot[0:ROWS, :], keys[index], values[index], None, outs[index])


def serve(slots, kv_cache, after):
    count = len(slots)
    return pl.pallas_call(
        functools.partial(serve_kernel, count),
        out_shape=[jax.ShapeDtypeStruct((SLOT, HD), jnp.bfloat16)] * count,
        in_specs=[vmem] * count + [hbm] + [anywhere] * len(after),
        out_specs=[vmem] * count,
        scratch_shapes=[
            pltpu.VMEM((count, BLK, HD), jnp.bfloat16),
            pltpu.VMEM((count, BLK, HD), jnp.bfloat16),
            pltpu.SemaphoreType.DMA((2, count)),
        ],
        compiler_params=params(),
        cost_estimate=pl.CostEstimate(flops=1 << 36, bytes_accessed=1 << 30, transcendentals=1),
        name="serve_slots",
    )(*slots, kv_cache, *after)


def serve_group_kernel(slots_ref, kv_ref, *refs):
    out_ref, keys, values, sems = refs[-4:]
    copies = []
    for place in range(NEAR):
        number = jnp.max(slots_ref[place, ROWS:SLOT, :].astype(jnp.float32)).astype(jnp.int32)
        start = pl.multiple_of(number * BLK, BLK)
        for half, buffer in enumerate((keys, values)):
            copy = pltpu.make_async_copy(
                kv_ref.at[half, pl.ds(start, BLK)], buffer.at[place], sems.at[half, place]
            )
            copy.start()
            copies.append(copy)
    for place in range(NEAR):
        copies[2 * place].wait()
        copies[2 * place + 1].wait()
        attend(slots_ref[place, 0:ROWS, :], keys[place], values[place], None, out_ref.at[place])


def serve_group(slots, kv_cache, after):
    return pl.pallas_call(
        serve_group_kernel,
        out_shape=jax.ShapeDtypeStruct((NEAR, SLOT, HD), jnp.bfloat16),
        in_specs=[vmem, hbm] + [anywhere] * len(after),
        out_specs=vmem,
        scratch_shapes=[
            pltpu.VMEM((NEAR, BLK, HD), jnp.bfloat16),
            pltpu.VMEM((NEAR, BLK, HD), jnp.bfloat16),
            pltpu.SemaphoreType.DMA((2, NEAR)),
        ],
        compiler_params=params(),
        cost_estimate=pl.CostEstimate(flops=1 << 36, bytes_accessed=1 << 30, transcendentals=1),
        name="serve_group",
    )(slots, kv_cache, *after)


def levels_of(parts):
    parts = parts.astype(jnp.float32)
    return parts[0:GROUP] + parts[GROUP : 2 * GROUP] + parts[2 * GROUP : 3 * GROUP]


def combine_kernel(tiles, blocks, seq_count, me_ref, selected_ref, own_ref, near_ref, *refs):
    far_refs, out_ref, blend = refs[: seq_count - NEAR], refs[-2], refs[-1]
    slots, routes = [], []
    for place in range(NEAR):
        slots.append(near_ref.at[place])
        routes.append(
            route(selected_ref, me_ref[0], (me_ref[0] & ~(NEAR - 1)) + place, tiles, blocks)
        )
    for index, slot in enumerate(far_refs):
        slots.append(slot)
        routes.append(route(selected_ref, me_ref[0], me_ref[0] ^ (NEAR + index), tiles, blocks))
    slot_levels = [levels_of(slot[ROWS:SLOT, :]) for slot in slots]
    for tile in range(tiles):
        own_level = levels_of(own_ref[tile, ROWS:SLOT, :])
        mine = [(filled > 0) & (number == tile) for number, _, filled in routes]
        levels = [own_level] + [
            jnp.where(used, level, -jnp.inf) for used, level in zip(mine, slot_levels)
        ]
        highest = functools.reduce(jnp.maximum, levels)
        factors = [jnp.exp(level - highest) for level in levels]
        norm = functools.reduce(jnp.add, factors)
        lines = jnp.concatenate([factor / norm for factor in factors], axis=0)
        count = lines.shape[0]
        room = -count % TILE
        if room:
            lines = jnp.concatenate([lines, jnp.zeros((room, TILE), jnp.float32)], axis=0)
        columns = jnp.concatenate(
            [lines[part * TILE : (part + 1) * TILE].T for part in range(lines.shape[0] // TILE)],
            axis=1,
        )
        for head in range(GROUP):
            part = slice(head * TILE, (head + 1) * TILE)
            blend[part, :] = columns[:, head : head + 1] * own_ref[tile, part, :].astype(jnp.float32)
        for index, used in enumerate(mine):

            @pl.when(used)
            def _(index=index, columns=columns):
                for head in range(GROUP):
                    part = slice(head * TILE, (head + 1) * TILE)
                    column = (index + 1) * GROUP + head
                    blend[part, :] += columns[:, column : column + 1] * slots[index][part, :].astype(
                        jnp.float32
                    )

        for head in range(GROUP):
            out_ref[tile * TILE : (tile + 1) * TILE, head * HD : (head + 1) * HD] = blend[
                head * TILE : (head + 1) * TILE, :
            ].astype(jnp.bfloat16)


def combine(me, selected, own, near, far, blocks, after):
    tiles, seq_count = own.shape[0], NEAR + len(far)
    return pl.pallas_call(
        functools.partial(combine_kernel, tiles, blocks, seq_count),
        out_shape=jax.ShapeDtypeStruct((tiles * TILE, GROUP * HD), jnp.bfloat16),
        in_specs=[smem, smem, vmem, vmem] + [vmem] * len(far) + [anywhere] * len(after),
        out_specs=vmem,
        scratch_shapes=[pltpu.VMEM((ROWS, HD), jnp.float32)],
        compiler_params=params(),
        cost_estimate=pl.CostEstimate(flops=1 << 36, bytes_accessed=1 << 30, transcendentals=1),
        name="combine_pieces",
    )(me, selected, own, near, *far, *after)


def project_kernel(heads, me_ref, *refs):
    attentions = refs[:heads]
    stack, stack_z, stack_x, whole_ref, share_ref, rest_ref = refs[heads:]
    depth = attentions[0].shape[1]
    z, h = me_ref[0], me_ref[2]
    lefts = []
    for index in range(heads):
        place = (z ^ index) ^ h
        left = attentions[0][...]
        for other in range(1, heads):
            left = jnp.where(place == other, attentions[other][...], left)
        lefts.append(left)
    near, rest = jnp.concatenate(lefts[0::2], axis=1), jnp.concatenate(lefts[1::2], axis=1)
    rest_ref[...] = rest
    share_ref[...] = jnp.dot(near, stack_x[...], preferred_element_type=jnp.float32)
    whole_ref[...] = (
        jnp.dot(near, stack[...], preferred_element_type=jnp.float32)
        + jnp.dot(rest, stack_z[...], preferred_element_type=jnp.float32)
    ).astype(jnp.bfloat16)


def finish_kernel(me_ref, rest_ref, stack_ref, share_ref, whole_ref, out_ref):
    width = whole_ref.shape[1]
    x = me_ref[1]
    total = share_ref[...] + jnp.dot(
        rest_ref[...], stack_ref[...], preferred_element_type=jnp.float32
    )
    out_ref[:, pl.ds(pl.multiple_of(x * width, width), width)] = whole_ref[...]
    out_ref[:, pl.ds(pl.multiple_of((x ^ 1) * width, width), width)] = total.astype(jnp.bfloat16)


def project(numbers, attentions, stacks):
    rows, width = attentions[0].shape[0], stacks[0].shape[1]
    heads = len(attentions)
    whole, share, rest = pl.pallas_call(
        functools.partial(project_kernel, heads),
        out_shape=[
            jax.ShapeDtypeStruct((rows, width), jnp.bfloat16),
            jax.ShapeDtypeStruct((rows, width), jnp.float32),
            jax.ShapeDtypeStruct((rows, stacks[3].shape[0]), jnp.bfloat16),
        ],
        in_specs=[smem] + [vmem] * (heads + 3),
        out_specs=[vmem] * 3,
        compiler_params=params(),
        name="project",
    )(numbers, *attentions, *stacks[:3])
    return pl.pallas_call(
        finish_kernel,
        out_shape=jax.ShapeDtypeStruct((rows, 2 * width), jnp.bfloat16),
        in_specs=[smem] + [vmem] * 4,
        out_specs=vmem,
        compiler_params=params(),
        name="finish",
    )(numbers, rest, stacks[3], share, whole)


def gate_kernel(*refs):
    del refs


def gate(array, *after):
    return pl.pallas_call(
        gate_kernel,
        out_shape=jax.ShapeDtypeStruct(array.shape, array.dtype),
        in_specs=[anywhere] * (1 + len(after)),
        out_specs=anywhere,
        input_output_aliases={0: 0},
        compiler_params=params(),
        cost_estimate=pl.CostEstimate(flops=1 << 36, bytes_accessed=1 << 30, transcendentals=1),
        name="gate",
    )(array, *after)


def pairs(count, offset):
    return [(index, index ^ offset) for index in range(count)]


def jump(weight, kvh_count, flip):
    moves = []
    for z in range(kvh_count):
        for x in range(2):
            for h in range(kvh_count):
                moves.append(((z * 2 + x) * kvh_count + h, ((h ^ flip) * 2 + x) * kvh_count + z))
    return lax.ppermute(weight, ("seq", "kvh"), moves)


def per_device(queries, kv_cache, selected, out_weight):
    seq_count, kvh_count = lax.axis_size("seq"), lax.axis_size("kvh")
    seq, kvh = lax.axis_index("seq"), lax.axis_index("kvh")
    blocks = kv_cache.shape[1] // BLK
    me = seq.astype(jnp.int32).reshape(1)
    requests = selected
    fast = seq_count == 2 * kvh_count and kvh_count == 4

    def move(array, offset):
        return lax.ppermute(array, "seq", pairs(seq_count, offset))

    stack = stack_z = stack_x = stack_zx = None
    if fast:
        jumps = [jump(out_weight, kvh_count, 0), jump(out_weight, kvh_count, 2)]
    if fast:
        stack = jnp.concatenate(jumps, axis=0)
        stack_z = move(stack, 2)
        stack_x = move(stack, 1)
    groups = [list(range(base, base + NEAR)) for base in range(0, seq_count, NEAR)]

    def swap(array):
        return lax.all_to_all(
            array, "seq", split_axis=0, concat_axis=0, axis_index_groups=groups, tiled=True
        )

    near, *far = pack(me, requests, queries, seq_count, blocks)
    arrived = {NEAR + index: move(slot, NEAR + index) for index, slot in enumerate(far)}
    returned = {}

    def answer(offsets, after):
        answers = serve([arrived[offset] for offset in offsets], kv_cache, after)
        for offset, result in zip(offsets, answers):
            returned[offset] = move(result, offset)
        return answers[-1]

    own = own_pieces(queries, kv_cache, [near])
    near_answers = serve_group(swap(near), kv_cache, [own] + [])
    returned_near = swap(near_answers)
    half = (seq_count + NEAR) // 2
    first = answer(list(range(NEAR, half)), [own] + ([stack] if fast else []))
    last = answer(list(range(half, seq_count)), [first] + [])
    if fast:
        stack_z = gate(stack_z, last)
        stack_zx = move(stack_z, 1)
    tick = gate(last, returned_near, *[returned[offset] for offset in range(NEAR, half)], *([stack_x] if fast else []))
    far = [returned[offset] for offset in range(NEAR, seq_count)]
    attention = combine(me, requests, own, returned_near, far, blocks, [tick] + [])
    if fast:
        other_y = lax.ppermute(attention, "kvh", pairs(kvh_count, 2))
        other_core = lax.ppermute(attention, "kvh", pairs(kvh_count, 1))
        both = lax.ppermute(other_y, "kvh", pairs(kvh_count, 1))
        gathered = [attention, other_core, other_y, both]
        stacks = [stack, stack_z, stack_x, stack_zx]
        numbers = jnp.stack([lax.shift_right_logical(seq, 1), seq & 1, kvh]).astype(jnp.int32)
        return project(numbers, gathered, stacks)
    column_terms = jnp.dot(
        attention,
        lax.all_gather(out_weight, "seq", axis=1, tiled=True),
        preferred_element_type=jnp.float32,
    )
    return lax.psum_scatter(
        column_terms.astype(jnp.bfloat16), "kvh", scatter_dimension=1, tiled=True
    )


def solution(mesh):
    in_specs = (P("seq", "kvh"), P(None, "seq", "kvh"), P("seq", "kvh", None), P("kvh", "seq"))
    out_specs = P("seq", "kvh")
    return jax.shard_map(
        per_device, mesh=mesh, in_specs=in_specs, out_specs=out_specs, check_vma=False
    )
```

```python
import functools
import math

import jax
import jax.numpy as jnp
from jax import lax
from jax.experimental import pallas as pl
from jax.experimental.pallas import tpu as pltpu
from jax.sharding import PartitionSpec as P

GROUP = 4
HD = 128
BLK = 1024
TILE = 128
SEL = 2
ROWS = GROUP * TILE
SLOT = ROWS + 16
NEAR = 4
SCALE = HD ** (-0.5)
LOG2E = math.log2(math.e)
VMEM_LIMIT = 48 * 1024 * 1024

vmem = pl.BlockSpec(memory_space=pltpu.VMEM)
smem = pl.BlockSpec(memory_space=pltpu.SMEM)
hbm = pl.BlockSpec(memory_space=pltpu.HBM)
anywhere = pl.BlockSpec(memory_space=pl.ANY)


def params():
    return pltpu.CompilerParams(vmem_limit_bytes=VMEM_LIMIT)


def route(selected_ref, own_seq, peer, tiles, blocks):
    own_block = own_seq * blocks + blocks - 1
    tile, block, filled = jnp.int32(0), jnp.int32(0), jnp.int32(0)
    for request in range(tiles * SEL):
        chosen = selected_ref[request // SEL, 0, request % SEL]
        target = jnp.where(chosen >= own_block, chosen + 1, chosen)
        here = lax.div(target, jnp.int32(blocks)) == peer
        tile = jnp.where(here, request // SEL, tile)
        block = jnp.where(here, lax.rem(target, jnp.int32(blocks)), block)
        filled = jnp.where(here, 1, filled)
    return tile, block, filled


def pack_kernel(tiles, blocks, me_ref, selected_ref, query_ref, near_ref, *far_refs):
    def fill(slot, peer):
        tile, block, _ = route(selected_ref, me_ref[0], peer, tiles, blocks)
        rows = pl.ds(pl.multiple_of(tile * TILE, TILE), TILE)
        for head in range(GROUP):
            slot[head * TILE : (head + 1) * TILE, :] = query_ref[rows, head * HD : (head + 1) * HD]
        slot[ROWS:SLOT, :] = jnp.full((16, HD), block.astype(jnp.float32)).astype(jnp.bfloat16)

    for place in range(NEAR):
        fill(near_ref.at[place], (me_ref[0] & ~(NEAR - 1)) + place)
    for index, slot in enumerate(far_refs):
        fill(slot, me_ref[0] ^ (NEAR + index))


def pack(me, selected, queries, seq_count, blocks):
    tiles = queries.shape[0] // TILE
    return pl.pallas_call(
        functools.partial(pack_kernel, tiles, blocks),
        out_shape=[jax.ShapeDtypeStruct((NEAR, SLOT, HD), jnp.bfloat16)]
        + [jax.ShapeDtypeStruct((SLOT, HD), jnp.bfloat16)] * (seq_count - NEAR),
        in_specs=[smem, smem, vmem],
        out_specs=[vmem] * (seq_count - NEAR + 1),
        compiler_params=params(),
        name="pack_queries",
    )(me, selected, queries)


def attend(query, keys, values, first_offset, out_ref):
    scores = lax.dot_general(
        query, keys, (((1,), (1,)), ((), ())), preferred_element_type=jnp.float32
    )
    if first_offset is not None:
        offsets = first_offset + lax.rem(
            lax.broadcasted_iota(jnp.int32, (ROWS, BLK), 0), jnp.int32(TILE)
        )
        seen = lax.broadcasted_iota(jnp.int32, (ROWS, BLK), 1) <= offsets
        scores = jnp.where(seen, scores, -jnp.inf)
    top = jnp.max(scores, axis=1, keepdims=True)
    weights = jnp.exp2((scores - top) * (SCALE * LOG2E))
    total = jnp.sum(weights, axis=1, keepdims=True)
    summed = jnp.dot(weights.astype(jnp.bfloat16), values, preferred_element_type=jnp.float32)
    out_ref[0:ROWS, :] = (summed / total).astype(jnp.bfloat16)
    level = top * SCALE + jnp.log(total)
    lane = lax.rem(lax.broadcasted_iota(jnp.int32, (TILE, TILE), 1), jnp.int32(GROUP))
    spread = jnp.zeros((TILE, TILE), jnp.float32)
    for head in range(GROUP):
        spread = jnp.where(lane == head, level[head * TILE : (head + 1) * TILE], spread)
    lines = spread.T[0:16]
    high = lines.astype(jnp.bfloat16).astype(jnp.float32)
    middle = (lines - high).astype(jnp.bfloat16).astype(jnp.float32)
    low = lines - high - middle
    row = lax.broadcasted_iota(jnp.int32, (16, TILE), 0)
    parts = jnp.where(row < GROUP, high, jnp.where(row < 2 * GROUP, middle, low))
    out_ref[ROWS:SLOT, :] = parts.astype(jnp.bfloat16)


def own_kernel(tiles, blocks, query_ref, kv_ref, *refs):
    out_ref, keys, values, sems = refs[-4:]
    start = (blocks - 1) * BLK
    copies = [
        pltpu.make_async_copy(kv_ref.at[0, pl.ds(start, BLK)], keys, sems.at[0]),
        pltpu.make_async_copy(kv_ref.at[1, pl.ds(start, BLK)], values, sems.at[1]),
    ]
    for copy in copies:
        copy.start()
    for copy in copies:
        copy.wait()

    def one(tile, carry):
        rows = pl.ds(pl.multiple_of(tile * TILE, TILE), TILE)
        query = jnp.concatenate(
            [query_ref[rows, head * HD : (head + 1) * HD] for head in range(GROUP)], axis=0
        )
        first_offset = BLK - tiles * TILE + tile * TILE
        attend(query, keys[...], values[...], first_offset, out_ref.at[tile])
        return carry

    lax.fori_loop(0, tiles, one, 0)


def own_pieces(queries, kv_cache, after):
    tiles, blocks = queries.shape[0] // TILE, kv_cache.shape[1] // BLK
    return pl.pallas_call(
        functools.partial(own_kernel, tiles, blocks),
        out_shape=jax.ShapeDtypeStruct((tiles, SLOT, HD), jnp.bfloat16),
        in_specs=[vmem, hbm] + [anywhere] * len(after),
        out_specs=vmem,
        scratch_shapes=[
            pltpu.VMEM((BLK, HD), jnp.bfloat16),
            pltpu.VMEM((BLK, HD), jnp.bfloat16),
            pltpu.SemaphoreType.DMA((2,)),
        ],
        compiler_params=params(),
        cost_estimate=pl.CostEstimate(flops=1 << 36, bytes_accessed=1 << 30, transcendentals=1),
        name="own_pieces",
    )(queries, kv_cache, *after)


def serve_kernel(count, *refs):
    slots, kv_ref, outs = refs[:count], refs[count], refs[-count - 3 : -3]
    keys, values, sems = refs[-3:]
    copies = []
    for index, slot in enumerate(slots):
        number = jnp.max(slot[ROWS:SLOT, :].astype(jnp.float32)).astype(jnp.int32)
        start = pl.multiple_of(number * BLK, BLK)
        for half, buffer in enumerate((keys, values)):
            copy = pltpu.make_async_copy(
                kv_ref.at[half, pl.ds(start, BLK)], buffer.at[index], sems.at[half, index]
            )
            copy.start()
            copies.append(copy)
    for index, slot in enumerate(slots):
        copies[2 * index].wait()
        copies[2 * index + 1].wait()
        attend(slot[0:ROWS, :], keys[index], values[index], None, outs[index])


def serve(slots, kv_cache, after):
    count = len(slots)
    return pl.pallas_call(
        functools.partial(serve_kernel, count),
        out_shape=[jax.ShapeDtypeStruct((SLOT, HD), jnp.bfloat16)] * count,
        in_specs=[vmem] * count + [hbm] + [anywhere] * len(after),
        out_specs=[vmem] * count,
        scratch_shapes=[
            pltpu.VMEM((count, BLK, HD), jnp.bfloat16),
            pltpu.VMEM((count, BLK, HD), jnp.bfloat16),
            pltpu.SemaphoreType.DMA((2, count)),
        ],
        compiler_params=params(),
        cost_estimate=pl.CostEstimate(flops=1 << 36, bytes_accessed=1 << 30, transcendentals=1),
        name="serve_slots",
    )(*slots, kv_cache, *after)


def serve_group_kernel(slots_ref, kv_ref, *refs):
    out_ref, keys, values, sems = refs[-4:]
    copies = []
    for place in range(NEAR):
        number = jnp.max(slots_ref[place, ROWS:SLOT, :].astype(jnp.float32)).astype(jnp.int32)
        start = pl.multiple_of(number * BLK, BLK)
        for half, buffer in enumerate((keys, values)):
            copy = pltpu.make_async_copy(
                kv_ref.at[half, pl.ds(start, BLK)], buffer.at[place], sems.at[half, place]
            )
            copy.start()
            copies.append(copy)
    for place in range(NEAR):
        copies[2 * place].wait()
        copies[2 * place + 1].wait()
        attend(slots_ref[place, 0:ROWS, :], keys[place], values[place], None, out_ref.at[place])


def serve_group(slots, kv_cache, after):
    return pl.pallas_call(
        serve_group_kernel,
        out_shape=jax.ShapeDtypeStruct((NEAR, SLOT, HD), jnp.bfloat16),
        in_specs=[vmem, hbm] + [anywhere] * len(after),
        out_specs=vmem,
        scratch_shapes=[
            pltpu.VMEM((NEAR, BLK, HD), jnp.bfloat16),
            pltpu.VMEM((NEAR, BLK, HD), jnp.bfloat16),
            pltpu.SemaphoreType.DMA((2, NEAR)),
        ],
        compiler_params=params(),
        cost_estimate=pl.CostEstimate(flops=1 << 36, bytes_accessed=1 << 30, transcendentals=1),
        name="serve_group",
    )(slots, kv_cache, *after)


def levels_of(parts):
    parts = parts.astype(jnp.float32)
    return parts[0:GROUP] + parts[GROUP : 2 * GROUP] + parts[2 * GROUP : 3 * GROUP]


def combine_kernel(tiles, blocks, seq_count, me_ref, selected_ref, own_ref, near_ref, *refs):
    far_refs, out_ref, blend = refs[: seq_count - NEAR], refs[-2], refs[-1]
    slots, routes = [], []
    for place in range(NEAR):
        slots.append(near_ref.at[place])
        routes.append(
            route(selected_ref, me_ref[0], (me_ref[0] & ~(NEAR - 1)) + place, tiles, blocks)
        )
    for index, slot in enumerate(far_refs):
        slots.append(slot)
        routes.append(route(selected_ref, me_ref[0], me_ref[0] ^ (NEAR + index), tiles, blocks))
    slot_levels = [levels_of(slot[ROWS:SLOT, :]) for slot in slots]
    for tile in range(tiles):
        own_level = levels_of(own_ref[tile, ROWS:SLOT, :])
        mine = [(filled > 0) & (number == tile) for number, _, filled in routes]
        levels = [own_level] + [
            jnp.where(used, level, -jnp.inf) for used, level in zip(mine, slot_levels)
        ]
        highest = functools.reduce(jnp.maximum, levels)
        factors = [jnp.exp(level - highest) for level in levels]
        norm = functools.reduce(jnp.add, factors)
        lines = jnp.concatenate([factor / norm for factor in factors], axis=0)
        count = lines.shape[0]
        room = -count % TILE
        if room:
            lines = jnp.concatenate([lines, jnp.zeros((room, TILE), jnp.float32)], axis=0)
        columns = jnp.concatenate(
            [lines[part * TILE : (part + 1) * TILE].T for part in range(lines.shape[0] // TILE)],
            axis=1,
        )
        for head in range(GROUP):
            part = slice(head * TILE, (head + 1) * TILE)
            blend[part, :] = columns[:, head : head + 1] * own_ref[tile, part, :].astype(jnp.float32)
        for index, used in enumerate(mine):

            @pl.when(used)
            def _(index=index, columns=columns):
                for head in range(GROUP):
                    part = slice(head * TILE, (head + 1) * TILE)
                    column = (index + 1) * GROUP + head
                    blend[part, :] += columns[:, column : column + 1] * slots[index][part, :].astype(
                        jnp.float32
                    )

        for head in range(GROUP):
            out_ref[tile * TILE : (tile + 1) * TILE, head * HD : (head + 1) * HD] = blend[
                head * TILE : (head + 1) * TILE, :
            ].astype(jnp.bfloat16)


def combine(me, selected, own, near, far, blocks, after):
    tiles, seq_count = own.shape[0], NEAR + len(far)
    return pl.pallas_call(
        functools.partial(combine_kernel, tiles, blocks, seq_count),
        out_shape=jax.ShapeDtypeStruct((tiles * TILE, GROUP * HD), jnp.bfloat16),
        in_specs=[smem, smem, vmem, vmem] + [vmem] * len(far) + [anywhere] * len(after),
        out_specs=vmem,
        scratch_shapes=[pltpu.VMEM((ROWS, HD), jnp.float32)],
        compiler_params=params(),
        cost_estimate=pl.CostEstimate(flops=1 << 36, bytes_accessed=1 << 30, transcendentals=1),
        name="combine_pieces",
    )(me, selected, own, near, *far, *after)


def project_kernel(heads, me_ref, *refs):
    attentions = refs[:heads]
    stack, stack_z, stack_x, whole_ref, share_ref, rest_ref = refs[heads:]
    depth = attentions[0].shape[1]
    z, h = me_ref[0], me_ref[2]
    lefts = []
    for index in range(heads):
        place = (z ^ index) ^ h
        left = attentions[0][...]
        for other in range(1, heads):
            left = jnp.where(place == other, attentions[other][...], left)
        lefts.append(left)
    near, rest = jnp.concatenate(lefts[0::2], axis=1), jnp.concatenate(lefts[1::2], axis=1)
    rest_ref[...] = rest
    share_ref[...] = jnp.dot(near, stack_x[...], preferred_element_type=jnp.float32)
    whole_ref[...] = (
        jnp.dot(near, stack[...], preferred_element_type=jnp.float32)
        + jnp.dot(rest, stack_z[...], preferred_element_type=jnp.float32)
    ).astype(jnp.bfloat16)


def finish_kernel(me_ref, rest_ref, first_ref, second_ref, share_ref, whole_ref, out_ref):
    depth, width = first_ref.shape
    x = me_ref[1]
    total = (
        share_ref[...]
        + jnp.dot(rest_ref[:, :depth], first_ref[...], preferred_element_type=jnp.float32)
        + jnp.dot(rest_ref[:, depth:], second_ref[...], preferred_element_type=jnp.float32)
    )
    out_ref[:, pl.ds(pl.multiple_of(x * width, width), width)] = whole_ref[...]
    out_ref[:, pl.ds(pl.multiple_of((x ^ 1) * width, width), width)] = total.astype(jnp.bfloat16)


def project(numbers, attentions, stacks):
    rows, width = attentions[0].shape[0], stacks[0].shape[1]
    heads = len(attentions)
    whole, share, rest = pl.pallas_call(
        functools.partial(project_kernel, heads),
        out_shape=[
            jax.ShapeDtypeStruct((rows, width), jnp.bfloat16),
            jax.ShapeDtypeStruct((rows, width), jnp.float32),
            jax.ShapeDtypeStruct((rows, 2 * stacks[3].shape[0]), jnp.bfloat16),
        ],
        in_specs=[smem] + [vmem] * (heads + 3),
        out_specs=[vmem] * 3,
        compiler_params=params(),
        name="project",
    )(numbers, *attentions, *stacks[:3])
    return pl.pallas_call(
        finish_kernel,
        out_shape=jax.ShapeDtypeStruct((rows, 2 * width), jnp.bfloat16),
        in_specs=[smem] + [vmem] * 5,
        out_specs=vmem,
        compiler_params=params(),
        name="finish",
    )(numbers, rest, stacks[3], stacks[4], share, whole)


def gate_kernel(*refs):
    del refs


def gate(array, *after):
    return pl.pallas_call(
        gate_kernel,
        out_shape=jax.ShapeDtypeStruct(array.shape, array.dtype),
        in_specs=[anywhere] * (1 + len(after)),
        out_specs=anywhere,
        input_output_aliases={0: 0},
        compiler_params=params(),
        cost_estimate=pl.CostEstimate(flops=1 << 36, bytes_accessed=1 << 30, transcendentals=1),
        name="gate",
    )(array, *after)


def pairs(count, offset):
    return [(index, index ^ offset) for index in range(count)]


def jump(weight, kvh_count, flip):
    moves = []
    for z in range(kvh_count):
        for x in range(2):
            for h in range(kvh_count):
                moves.append(((z * 2 + x) * kvh_count + h, ((h ^ flip) * 2 + x) * kvh_count + z))
    return lax.ppermute(weight, ("seq", "kvh"), moves)


def per_device(queries, kv_cache, selected, out_weight):
    seq_count, kvh_count = lax.axis_size("seq"), lax.axis_size("kvh")
    seq, kvh = lax.axis_index("seq"), lax.axis_index("kvh")
    blocks = kv_cache.shape[1] // BLK
    me = seq.astype(jnp.int32).reshape(1)
    requests = selected
    fast = seq_count == 2 * kvh_count and kvh_count == 4

    def move(array, offset):
        return lax.ppermute(array, "seq", pairs(seq_count, offset))

    stack = stack_z = stack_x = None
    if fast:
        jumps = [jump(out_weight, kvh_count, 0), jump(out_weight, kvh_count, 2)]
    if fast:
        stack = jnp.concatenate(jumps, axis=0)
        stack_z = move(stack, 2)
        stack_x = move(stack, 1)
    groups = [list(range(base, base + NEAR)) for base in range(0, seq_count, NEAR)]

    def swap(array):
        return lax.all_to_all(
            array, "seq", split_axis=0, concat_axis=0, axis_index_groups=groups, tiled=True
        )

    near, *far = pack(me, requests, queries, seq_count, blocks)
    arrived = {NEAR + index: move(slot, NEAR + index) for index, slot in enumerate(far)}
    returned = {}

    def answer(offsets, after):
        answers = serve([arrived[offset] for offset in offsets], kv_cache, after)
        for offset, result in zip(offsets, answers):
            returned[offset] = move(result, offset)
        return answers[-1]

    own = own_pieces(queries, kv_cache, [near])
    near_answers = serve_group(swap(near), kv_cache, [own] + [])
    returned_near = swap(near_answers)
    half = (seq_count + NEAR) // 2
    first = answer(list(range(NEAR, half)), [own] + ([stack] if fast else []))
    last = answer(list(range(half, seq_count)), [first] + [])
    if fast:
        depth = out_weight.shape[0]
        first_zx = move(gate(stack_z[:depth], near_answers), 1)
        second_zx = move(gate(stack_x[depth:], near_answers), 2)
    tick = gate(last, returned_near, *[returned[offset] for offset in range(NEAR, half)], *([stack_x] if fast else []))
    far = [returned[offset] for offset in range(NEAR, seq_count)]
    attention = combine(me, requests, own, returned_near, far, blocks, [tick] + [])
    if fast:
        other_y = lax.ppermute(attention, "kvh", pairs(kvh_count, 2))
        other_core = lax.ppermute(attention, "kvh", pairs(kvh_count, 1))
        both = lax.ppermute(other_y, "kvh", pairs(kvh_count, 1))
        gathered = [attention, other_core, other_y, both]
        stacks = [stack, stack_z, stack_x, first_zx, second_zx]
        numbers = jnp.stack([lax.shift_right_logical(seq, 1), seq & 1, kvh]).astype(jnp.int32)
        return project(numbers, gathered, stacks)
    column_terms = jnp.dot(
        attention,
        lax.all_gather(out_weight, "seq", axis=1, tiled=True),
        preferred_element_type=jnp.float32,
    )
    return lax.psum_scatter(
        column_terms.astype(jnp.bfloat16), "kvh", scatter_dimension=1, tiled=True
    )


def solution(mesh):
    in_specs = (P("seq", "kvh"), P(None, "seq", "kvh"), P("seq", "kvh", None), P("kvh", "seq"))
    out_specs = P("seq", "kvh")
    return jax.shard_map(
        per_device, mesh=mesh, in_specs=in_specs, out_specs=out_specs, check_vma=False
    )
```

```python
import functools
import math

import jax
import jax.numpy as jnp
from jax import lax
from jax.experimental import pallas as pl
from jax.experimental.pallas import tpu as pltpu
from jax.sharding import PartitionSpec as P

GROUP = 4
HD = 128
BLK = 1024
TILE = 128
SEL = 2
ROWS = GROUP * TILE
SLOT = ROWS + 16
NEAR = 4
SCALE = HD ** (-0.5)
LOG2E = math.log2(math.e)
VMEM_LIMIT = 48 * 1024 * 1024

vmem = pl.BlockSpec(memory_space=pltpu.VMEM)
smem = pl.BlockSpec(memory_space=pltpu.SMEM)
hbm = pl.BlockSpec(memory_space=pltpu.HBM)
anywhere = pl.BlockSpec(memory_space=pl.ANY)


def params():
    return pltpu.CompilerParams(vmem_limit_bytes=VMEM_LIMIT)


def route(selected_ref, own_seq, peer, tiles, blocks):
    own_block = own_seq * blocks + blocks - 1
    tile, block, filled = jnp.int32(0), jnp.int32(0), jnp.int32(0)
    for request in range(tiles * SEL):
        chosen = selected_ref[request // SEL, 0, request % SEL]
        target = jnp.where(chosen >= own_block, chosen + 1, chosen)
        here = lax.div(target, jnp.int32(blocks)) == peer
        tile = jnp.where(here, request // SEL, tile)
        block = jnp.where(here, lax.rem(target, jnp.int32(blocks)), block)
        filled = jnp.where(here, 1, filled)
    return tile, block, filled


def pack_kernel(tiles, blocks, me_ref, selected_ref, query_ref, near_ref, *far_refs):
    def fill(slot, peer):
        tile, block, _ = route(selected_ref, me_ref[0], peer, tiles, blocks)
        rows = pl.ds(pl.multiple_of(tile * TILE, TILE), TILE)
        for head in range(GROUP):
            slot[head * TILE : (head + 1) * TILE, :] = query_ref[rows, head * HD : (head + 1) * HD]
        slot[ROWS:SLOT, :] = jnp.full((16, HD), block.astype(jnp.float32)).astype(jnp.bfloat16)

    for place in range(NEAR):
        fill(near_ref.at[place], (me_ref[0] & ~(NEAR - 1)) + place)
    for index, slot in enumerate(far_refs):
        fill(slot, me_ref[0] ^ (NEAR + index))


def pack(me, selected, queries, seq_count, blocks):
    tiles = queries.shape[0] // TILE
    return pl.pallas_call(
        functools.partial(pack_kernel, tiles, blocks),
        out_shape=[jax.ShapeDtypeStruct((NEAR, SLOT, HD), jnp.bfloat16)]
        + [jax.ShapeDtypeStruct((SLOT, HD), jnp.bfloat16)] * (seq_count - NEAR),
        in_specs=[smem, smem, vmem],
        out_specs=[vmem] * (seq_count - NEAR + 1),
        compiler_params=params(),
        name="pack_queries",
    )(me, selected, queries)


def attend(query, keys, values, first_offset, out_ref):
    levels = []
    step = ROWS // 2
    for base in range(0, ROWS, step):
        scores = lax.dot_general(
            query[base : base + step], keys, (((1,), (1,)), ((), ())), preferred_element_type=jnp.float32
        )
        if first_offset is not None:
            offsets = first_offset + lax.rem(
                lax.broadcasted_iota(jnp.int32, (step, BLK), 0), jnp.int32(TILE)
            )
            seen = lax.broadcasted_iota(jnp.int32, (step, BLK), 1) <= offsets
            scores = jnp.where(seen, scores, -jnp.inf)
        top = jnp.max(scores, axis=1, keepdims=True)
        weights = jnp.exp2((scores - top) * (SCALE * LOG2E))
        total = jnp.sum(weights, axis=1, keepdims=True)
        summed = jnp.dot(weights.astype(jnp.bfloat16), values, preferred_element_type=jnp.float32)
        out_ref[base : base + step, :] = (summed / total).astype(jnp.bfloat16)
        levels.append(top * SCALE + jnp.log(total))
    level = jnp.concatenate(levels, axis=0)
    lane = lax.rem(lax.broadcasted_iota(jnp.int32, (TILE, TILE), 1), jnp.int32(GROUP))
    spread = jnp.zeros((TILE, TILE), jnp.float32)
    for head in range(GROUP):
        spread = jnp.where(lane == head, level[head * TILE : (head + 1) * TILE], spread)
    lines = spread.T[0:16]
    high = lines.astype(jnp.bfloat16).astype(jnp.float32)
    middle = (lines - high).astype(jnp.bfloat16).astype(jnp.float32)
    low = lines - high - middle
    row = lax.broadcasted_iota(jnp.int32, (16, TILE), 0)
    parts = jnp.where(row < GROUP, high, jnp.where(row < 2 * GROUP, middle, low))
    out_ref[ROWS:SLOT, :] = parts.astype(jnp.bfloat16)


def own_kernel(tiles, blocks, query_ref, kv_ref, *refs):
    out_ref, keys, values, sems = refs[-4:]
    start = (blocks - 1) * BLK
    copies = [
        pltpu.make_async_copy(kv_ref.at[0, pl.ds(start, BLK)], keys, sems.at[0]),
        pltpu.make_async_copy(kv_ref.at[1, pl.ds(start, BLK)], values, sems.at[1]),
    ]
    for copy in copies:
        copy.start()
    for copy in copies:
        copy.wait()

    def one(tile, carry):
        rows = pl.ds(pl.multiple_of(tile * TILE, TILE), TILE)
        query = jnp.concatenate(
            [query_ref[rows, head * HD : (head + 1) * HD] for head in range(GROUP)], axis=0
        )
        first_offset = BLK - tiles * TILE + tile * TILE
        attend(query, keys[...], values[...], first_offset, out_ref.at[tile])
        return carry

    lax.fori_loop(0, tiles, one, 0)


def own_pieces(queries, kv_cache, after):
    tiles, blocks = queries.shape[0] // TILE, kv_cache.shape[1] // BLK
    return pl.pallas_call(
        functools.partial(own_kernel, tiles, blocks),
        out_shape=jax.ShapeDtypeStruct((tiles, SLOT, HD), jnp.bfloat16),
        in_specs=[vmem, hbm] + [anywhere] * len(after),
        out_specs=vmem,
        scratch_shapes=[
            pltpu.VMEM((BLK, HD), jnp.bfloat16),
            pltpu.VMEM((BLK, HD), jnp.bfloat16),
            pltpu.SemaphoreType.DMA((2,)),
        ],
        compiler_params=params(),
        cost_estimate=pl.CostEstimate(flops=1 << 36, bytes_accessed=1 << 30, transcendentals=1),
        name="own_pieces",
    )(queries, kv_cache, *after)


def serve_kernel(count, *refs):
    slots, kv_ref, outs = refs[:count], refs[count], refs[-count - 3 : -3]
    keys, values, sems = refs[-3:]
    copies = []
    for index, slot in enumerate(slots):
        number = jnp.max(slot[ROWS:SLOT, :].astype(jnp.float32)).astype(jnp.int32)
        start = pl.multiple_of(number * BLK, BLK)
        for half, buffer in enumerate((keys, values)):
            copy = pltpu.make_async_copy(
                kv_ref.at[half, pl.ds(start, BLK)], buffer.at[index], sems.at[half, index]
            )
            copy.start()
            copies.append(copy)
    for index, slot in enumerate(slots):
        copies[2 * index].wait()
        copies[2 * index + 1].wait()
        attend(slot[0:ROWS, :], keys[index], values[index], None, outs[index])


def serve(slots, kv_cache, after):
    count = len(slots)
    return pl.pallas_call(
        functools.partial(serve_kernel, count),
        out_shape=[jax.ShapeDtypeStruct((SLOT, HD), jnp.bfloat16)] * count,
        in_specs=[vmem] * count + [hbm] + [anywhere] * len(after),
        out_specs=[vmem] * count,
        scratch_shapes=[
            pltpu.VMEM((count, BLK, HD), jnp.bfloat16),
            pltpu.VMEM((count, BLK, HD), jnp.bfloat16),
            pltpu.SemaphoreType.DMA((2, count)),
        ],
        compiler_params=params(),
        cost_estimate=pl.CostEstimate(flops=1 << 36, bytes_accessed=1 << 30, transcendentals=1),
        name="serve_slots",
    )(*slots, kv_cache, *after)


def serve_group_kernel(slots_ref, kv_ref, *refs):
    out_ref, keys, values, sems = refs[-4:]
    copies = []
    for place in range(NEAR):
        number = jnp.max(slots_ref[place, ROWS:SLOT, :].astype(jnp.float32)).astype(jnp.int32)
        start = pl.multiple_of(number * BLK, BLK)
        for half, buffer in enumerate((keys, values)):
            copy = pltpu.make_async_copy(
                kv_ref.at[half, pl.ds(start, BLK)], buffer.at[place], sems.at[half, place]
            )
            copy.start()
            copies.append(copy)
    for place in range(NEAR):
        copies[2 * place].wait()
        copies[2 * place + 1].wait()
        attend(slots_ref[place, 0:ROWS, :], keys[place], values[place], None, out_ref.at[place])


def serve_group(slots, kv_cache, after):
    return pl.pallas_call(
        serve_group_kernel,
        out_shape=jax.ShapeDtypeStruct((NEAR, SLOT, HD), jnp.bfloat16),
        in_specs=[vmem, hbm] + [anywhere] * len(after),
        out_specs=vmem,
        scratch_shapes=[
            pltpu.VMEM((NEAR, BLK, HD), jnp.bfloat16),
            pltpu.VMEM((NEAR, BLK, HD), jnp.bfloat16),
            pltpu.SemaphoreType.DMA((2, NEAR)),
        ],
        compiler_params=params(),
        cost_estimate=pl.CostEstimate(flops=1 << 36, bytes_accessed=1 << 30, transcendentals=1),
        name="serve_group",
    )(slots, kv_cache, *after)


def levels_of(parts):
    parts = parts.astype(jnp.float32)
    return parts[0:GROUP] + parts[GROUP : 2 * GROUP] + parts[2 * GROUP : 3 * GROUP]


def combine_kernel(tiles, blocks, seq_count, me_ref, selected_ref, own_ref, near_ref, *refs):
    far_refs, out_ref, blend = refs[: seq_count - NEAR], refs[-2], refs[-1]
    slots, routes = [], []
    for place in range(NEAR):
        slots.append(near_ref.at[place])
        routes.append(
            route(selected_ref, me_ref[0], (me_ref[0] & ~(NEAR - 1)) + place, tiles, blocks)
        )
    for index, slot in enumerate(far_refs):
        slots.append(slot)
        routes.append(route(selected_ref, me_ref[0], me_ref[0] ^ (NEAR + index), tiles, blocks))
    slot_levels = [levels_of(slot[ROWS:SLOT, :]) for slot in slots]
    for tile in range(tiles):
        own_level = levels_of(own_ref[tile, ROWS:SLOT, :])
        mine = [(filled > 0) & (number == tile) for number, _, filled in routes]
        levels = [own_level] + [
            jnp.where(used, level, -jnp.inf) for used, level in zip(mine, slot_levels)
        ]
        highest = functools.reduce(jnp.maximum, levels)
        factors = [jnp.exp(level - highest) for level in levels]
        norm = functools.reduce(jnp.add, factors)
        lines = jnp.concatenate([factor / norm for factor in factors], axis=0)
        count = lines.shape[0]
        room = -count % TILE
        if room:
            lines = jnp.concatenate([lines, jnp.zeros((room, TILE), jnp.float32)], axis=0)
        columns = jnp.concatenate(
            [lines[part * TILE : (part + 1) * TILE].T for part in range(lines.shape[0] // TILE)],
            axis=1,
        )
        for head in range(GROUP):
            part = slice(head * TILE, (head + 1) * TILE)
            blend[part, :] = columns[:, head : head + 1] * own_ref[tile, part, :].astype(jnp.float32)
        for index, used in enumerate(mine):

            @pl.when(used)
            def _(index=index, columns=columns):
                for head in range(GROUP):
                    part = slice(head * TILE, (head + 1) * TILE)
                    column = (index + 1) * GROUP + head
                    blend[part, :] += columns[:, column : column + 1] * slots[index][part, :].astype(
                        jnp.float32
                    )

        for head in range(GROUP):
            out_ref[tile * TILE : (tile + 1) * TILE, head * HD : (head + 1) * HD] = blend[
                head * TILE : (head + 1) * TILE, :
            ].astype(jnp.bfloat16)


def combine(me, selected, own, near, far, blocks, after):
    tiles, seq_count = own.shape[0], NEAR + len(far)
    return pl.pallas_call(
        functools.partial(combine_kernel, tiles, blocks, seq_count),
        out_shape=jax.ShapeDtypeStruct((tiles * TILE, GROUP * HD), jnp.bfloat16),
        in_specs=[smem, smem, vmem, vmem] + [vmem] * len(far) + [anywhere] * len(after),
        out_specs=vmem,
        scratch_shapes=[pltpu.VMEM((ROWS, HD), jnp.float32)],
        compiler_params=params(),
        cost_estimate=pl.CostEstimate(flops=1 << 36, bytes_accessed=1 << 30, transcendentals=1),
        name="combine_pieces",
    )(me, selected, own, near, *far, *after)


def halves(numbers_ref, first, second):
    even = ((numbers_ref[0] ^ numbers_ref[2]) & 1) == 0
    return jnp.where(even, first, second), jnp.where(even, second, first)


def project_kernel(numbers_ref, own_ref, core_ref, stack, stack_z, stack_x, whole_ref, share_ref):
    depth = own_ref.shape[1]
    part = lax.shift_right_logical(numbers_ref[0] ^ numbers_ref[2], 1)
    rows = pl.ds(pl.multiple_of(part * depth, depth), depth)
    even, odd = halves(numbers_ref, own_ref[...], core_ref[...])
    whole_ref[...] = jnp.dot(even, stack[rows, :], preferred_element_type=jnp.float32) + jnp.dot(
        odd, stack_z[rows, :], preferred_element_type=jnp.float32
    )
    share_ref[...] = jnp.dot(even, stack_x[rows, :], preferred_element_type=jnp.float32)


def finish_kernel(numbers_ref, own_ref, core_ref, y_ref, both_ref, *refs):
    stack, stack_z, stack_x, first_ref, second_ref, whole_ref, share_ref, out_ref = refs
    depth, width = first_ref.shape
    x = numbers_ref[1]
    part = lax.shift_right_logical(numbers_ref[0] ^ numbers_ref[2], 1)
    rows = pl.ds(pl.multiple_of((1 - part) * depth, depth), depth)
    _, near_odd = halves(numbers_ref, own_ref[...], core_ref[...])
    even, odd = halves(numbers_ref, y_ref[...], both_ref[...])
    whole = (
        whole_ref[...]
        + jnp.dot(even, stack[rows, :], preferred_element_type=jnp.float32)
        + jnp.dot(odd, stack_z[rows, :], preferred_element_type=jnp.float32)
    )
    share = (
        share_ref[...]
        + jnp.dot(even, stack_x[rows, :], preferred_element_type=jnp.float32)
        + jnp.dot(
            jnp.where(part == 0, near_odd, odd), first_ref[...], preferred_element_type=jnp.float32
        )
        + jnp.dot(
            jnp.where(part == 0, odd, near_odd), second_ref[...], preferred_element_type=jnp.float32
        )
    )
    out_ref[:, pl.ds(pl.multiple_of(x * width, width), width)] = whole.astype(jnp.bfloat16)
    out_ref[:, pl.ds(pl.multiple_of((x ^ 1) * width, width), width)] = share.astype(jnp.bfloat16)


def project(numbers, attentions, stacks):
    rows, width = attentions[0].shape[0], stacks[0].shape[1]
    return pl.pallas_call(
        project_kernel,
        out_shape=[jax.ShapeDtypeStruct((rows, width), jnp.float32)] * 2,
        in_specs=[smem] + [vmem] * 5,
        out_specs=[vmem] * 2,
        compiler_params=params(),
        name="project",
    )(numbers, *attentions, *stacks)


def finish(numbers, attentions, stacks, whole, share):
    rows, width = attentions[0].shape[0], stacks[0].shape[1]
    return pl.pallas_call(
        finish_kernel,
        out_shape=jax.ShapeDtypeStruct((rows, 2 * width), jnp.bfloat16),
        in_specs=[smem] + [vmem] * 11,
        out_specs=vmem,
        compiler_params=params(),
        name="finish",
    )(numbers, *attentions, *stacks, whole, share)


def gate_kernel(*refs):
    del refs


def gate(array, *after):
    return pl.pallas_call(
        gate_kernel,
        out_shape=jax.ShapeDtypeStruct(array.shape, array.dtype),
        in_specs=[anywhere] * (1 + len(after)),
        out_specs=anywhere,
        input_output_aliases={0: 0},
        compiler_params=params(),
        cost_estimate=pl.CostEstimate(flops=1 << 36, bytes_accessed=1 << 30, transcendentals=1),
        name="gate",
    )(array, *after)


def pairs(count, offset):
    return [(index, index ^ offset) for index in range(count)]


def jump(weight, kvh_count, flip):
    moves = []
    for z in range(kvh_count):
        for x in range(2):
            for h in range(kvh_count):
                moves.append(((z * 2 + x) * kvh_count + h, ((h ^ flip) * 2 + x) * kvh_count + z))
    return lax.ppermute(weight, ("seq", "kvh"), moves)


def per_device(queries, kv_cache, selected, out_weight):
    seq_count, kvh_count = lax.axis_size("seq"), lax.axis_size("kvh")
    seq, kvh = lax.axis_index("seq"), lax.axis_index("kvh")
    blocks = kv_cache.shape[1] // BLK
    me = seq.astype(jnp.int32).reshape(1)
    requests = selected
    fast = seq_count == 2 * kvh_count and kvh_count == 4

    def move(array, offset):
        return lax.ppermute(array, "seq", pairs(seq_count, offset))

    stack = stack_z = stack_x = None
    if fast:
        jumps = [jump(out_weight, kvh_count, 0), jump(out_weight, kvh_count, 2)]
    if fast:
        stack = jnp.concatenate(jumps, axis=0)
        stack_z = move(stack, 2)
        stack_x = move(stack, 1)
    groups = [list(range(base, base + NEAR)) for base in range(0, seq_count, NEAR)]

    def swap(array):
        return lax.all_to_all(
            array, "seq", split_axis=0, concat_axis=0, axis_index_groups=groups, tiled=True
        )

    near, *far = pack(me, requests, queries, seq_count, blocks)
    arrived = {NEAR + index: move(slot, NEAR + index) for index, slot in enumerate(far)}
    returned = {}

    def answer(offsets, after):
        answers = serve([arrived[offset] for offset in offsets], kv_cache, after)
        for offset, result in zip(offsets, answers):
            returned[offset] = move(result, offset)
        return answers[-1]

    own = own_pieces(queries, kv_cache, [near])
    near_answers = serve_group(swap(near), kv_cache, [own] + [])
    returned_near = swap(near_answers)
    half = (seq_count + NEAR) // 2
    first = answer(list(range(NEAR, half)), [own] + ([stack] if fast else []))
    last = answer(list(range(half, seq_count)), [first] + [])
    if fast:
        depth = out_weight.shape[0]
        first_zx = move(gate(stack_z[:depth], near_answers), 1)
        second_zx = move(gate(stack_x[depth:], near_answers), 2)
    tick = gate(last, returned_near, *[returned[offset] for offset in range(NEAR, half)], *([stack_x] if fast else []))
    far = [returned[offset] for offset in range(NEAR, seq_count)]
    attention = combine(me, requests, own, returned_near, far, blocks, [tick] + [])
    if fast:
        other_y = lax.ppermute(attention, "kvh", pairs(kvh_count, 2))
        other_core = lax.ppermute(attention, "kvh", pairs(kvh_count, 1))
        numbers = jnp.stack([lax.shift_right_logical(seq, 1), seq & 1, kvh]).astype(jnp.int32)
        stacks = [stack, stack_z, stack_x]
        whole, share = project(numbers, [attention, other_core], stacks)
        other_y = gate(other_y, whole, first_zx, second_zx)
        both = lax.ppermute(other_y, "kvh", pairs(kvh_count, 1))
        attentions = [attention, other_core, other_y, both]
        return finish(numbers, attentions, [*stacks, first_zx, second_zx], whole, share)
    column_terms = jnp.dot(
        attention,
        lax.all_gather(out_weight, "seq", axis=1, tiled=True),
        preferred_element_type=jnp.float32,
    )
    return lax.psum_scatter(
        column_terms.astype(jnp.bfloat16), "kvh", scatter_dimension=1, tiled=True
    )


def solution(mesh):
    in_specs = (P("seq", "kvh"), P(None, "seq", "kvh"), P("seq", "kvh", None), P("kvh", "seq"))
    out_specs = P("seq", "kvh")
    return jax.shard_map(
        per_device, mesh=mesh, in_specs=in_specs, out_specs=out_specs, check_vma=False
    )
```

```python
import functools
import math

import jax
import jax.numpy as jnp
from jax import lax
from jax.experimental import pallas as pl
from jax.experimental.pallas import tpu as pltpu
from jax.sharding import PartitionSpec as P

GROUP = 4
HD = 128
BLK = 1024
TILE = 128
SEL = 2
ROWS = GROUP * TILE
SLOT = ROWS + 16
NEAR = 4
SCALE = HD ** (-0.5)
LOG2E = math.log2(math.e)
VMEM_LIMIT = 48 * 1024 * 1024

vmem = pl.BlockSpec(memory_space=pltpu.VMEM)
smem = pl.BlockSpec(memory_space=pltpu.SMEM)
hbm = pl.BlockSpec(memory_space=pltpu.HBM)
anywhere = pl.BlockSpec(memory_space=pl.ANY)


def params():
    return pltpu.CompilerParams(vmem_limit_bytes=VMEM_LIMIT)


def route(selected_ref, own_seq, peer, tiles, blocks):
    own_block = own_seq * blocks + blocks - 1
    tile, block, filled = jnp.int32(0), jnp.int32(0), jnp.int32(0)
    for request in range(tiles * SEL):
        chosen = selected_ref[request // SEL, 0, request % SEL]
        target = jnp.where(chosen >= own_block, chosen + 1, chosen)
        here = lax.div(target, jnp.int32(blocks)) == peer
        tile = jnp.where(here, request // SEL, tile)
        block = jnp.where(here, lax.rem(target, jnp.int32(blocks)), block)
        filled = jnp.where(here, 1, filled)
    return tile, block, filled


def pack_kernel(tiles, blocks, me_ref, selected_ref, query_ref, near_ref, self_ref, *far_refs):
    def fill(slot, peer):
        tile, block, _ = route(selected_ref, me_ref[0], peer, tiles, blocks)
        rows = pl.ds(pl.multiple_of(tile * TILE, TILE), TILE)
        for head in range(GROUP):
            slot[head * TILE : (head + 1) * TILE, :] = query_ref[rows, head * HD : (head + 1) * HD]
        slot[ROWS:SLOT, :] = jnp.full((16, HD), block.astype(jnp.float32)).astype(jnp.bfloat16)

    for place in range(NEAR):
        fill(near_ref.at[place], (me_ref[0] & ~(NEAR - 1)) + place)
    fill(self_ref, me_ref[0])
    for index, slot in enumerate(far_refs):
        fill(slot, me_ref[0] ^ (NEAR + index))


def pack(me, selected, queries, seq_count, blocks):
    tiles = queries.shape[0] // TILE
    return pl.pallas_call(
        functools.partial(pack_kernel, tiles, blocks),
        out_shape=[jax.ShapeDtypeStruct((NEAR, SLOT, HD), jnp.bfloat16)]
        + [jax.ShapeDtypeStruct((SLOT, HD), jnp.bfloat16)] * (seq_count - NEAR + 1),
        in_specs=[smem, smem, vmem],
        out_specs=[vmem] * (seq_count - NEAR + 2),
        compiler_params=params(),
        name="pack_queries",
    )(me, selected, queries)


def attend(query, keys, values, first_offset, out_ref):
    levels = []
    step = ROWS // 2
    for base in range(0, ROWS, step):
        scores = lax.dot_general(
            query[base : base + step], keys, (((1,), (1,)), ((), ())), preferred_element_type=jnp.float32
        )
        if first_offset is not None:
            offsets = first_offset + lax.rem(
                lax.broadcasted_iota(jnp.int32, (step, BLK), 0), jnp.int32(TILE)
            )
            seen = lax.broadcasted_iota(jnp.int32, (step, BLK), 1) <= offsets
            scores = jnp.where(seen, scores, -jnp.inf)
        top = jnp.max(scores, axis=1, keepdims=True)
        weights = jnp.exp2((scores - top) * (SCALE * LOG2E))
        total = jnp.sum(weights, axis=1, keepdims=True)
        summed = jnp.dot(weights.astype(jnp.bfloat16), values, preferred_element_type=jnp.float32)
        out_ref[base : base + step, :] = (summed / total).astype(jnp.bfloat16)
        levels.append(top * SCALE + jnp.log(total))
    level = jnp.concatenate(levels, axis=0)
    lane = lax.rem(lax.broadcasted_iota(jnp.int32, (TILE, TILE), 1), jnp.int32(GROUP))
    spread = jnp.zeros((TILE, TILE), jnp.float32)
    for head in range(GROUP):
        spread = jnp.where(lane == head, level[head * TILE : (head + 1) * TILE], spread)
    lines = spread.T[0:16]
    high = lines.astype(jnp.bfloat16).astype(jnp.float32)
    middle = (lines - high).astype(jnp.bfloat16).astype(jnp.float32)
    low = lines - high - middle
    row = lax.broadcasted_iota(jnp.int32, (16, TILE), 0)
    parts = jnp.where(row < GROUP, high, jnp.where(row < 2 * GROUP, middle, low))
    out_ref[ROWS:SLOT, :] = parts.astype(jnp.bfloat16)


def own_kernel(tiles, blocks, query_ref, kv_ref, *refs):
    out_ref, keys, values, sems = refs[-4:]
    start = (blocks - 1) * BLK
    copies = [
        pltpu.make_async_copy(kv_ref.at[0, pl.ds(start, BLK)], keys, sems.at[0]),
        pltpu.make_async_copy(kv_ref.at[1, pl.ds(start, BLK)], values, sems.at[1]),
    ]
    for copy in copies:
        copy.start()
    for copy in copies:
        copy.wait()

    def one(tile, carry):
        rows = pl.ds(pl.multiple_of(tile * TILE, TILE), TILE)
        query = jnp.concatenate(
            [query_ref[rows, head * HD : (head + 1) * HD] for head in range(GROUP)], axis=0
        )
        first_offset = BLK - tiles * TILE + tile * TILE
        attend(query, keys[...], values[...], first_offset, out_ref.at[tile])
        return carry

    lax.fori_loop(0, tiles, one, 0)


def own_pieces(queries, kv_cache, after):
    tiles, blocks = queries.shape[0] // TILE, kv_cache.shape[1] // BLK
    return pl.pallas_call(
        functools.partial(own_kernel, tiles, blocks),
        out_shape=jax.ShapeDtypeStruct((tiles, SLOT, HD), jnp.bfloat16),
        in_specs=[vmem, hbm] + [anywhere] * len(after),
        out_specs=vmem,
        scratch_shapes=[
            pltpu.VMEM((BLK, HD), jnp.bfloat16),
            pltpu.VMEM((BLK, HD), jnp.bfloat16),
            pltpu.SemaphoreType.DMA((2,)),
        ],
        compiler_params=params(),
        cost_estimate=pl.CostEstimate(flops=1 << 36, bytes_accessed=1 << 30, transcendentals=1),
        name="own_pieces",
    )(queries, kv_cache, *after)


def serve_kernel(count, *refs):
    slots, kv_ref, outs = refs[:count], refs[count], refs[-count - 3 : -3]
    keys, values, sems = refs[-3:]
    copies = []
    for index, slot in enumerate(slots):
        number = jnp.max(slot[ROWS:SLOT, :].astype(jnp.float32)).astype(jnp.int32)
        start = pl.multiple_of(number * BLK, BLK)
        for half, buffer in enumerate((keys, values)):
            copy = pltpu.make_async_copy(
                kv_ref.at[half, pl.ds(start, BLK)], buffer.at[index], sems.at[half, index]
            )
            copy.start()
            copies.append(copy)
    for index, slot in enumerate(slots):
        copies[2 * index].wait()
        copies[2 * index + 1].wait()
        attend(slot[0:ROWS, :], keys[index], values[index], None, outs[index])


def serve(slots, kv_cache, after):
    count = len(slots)
    return pl.pallas_call(
        functools.partial(serve_kernel, count),
        out_shape=[jax.ShapeDtypeStruct((SLOT, HD), jnp.bfloat16)] * count,
        in_specs=[vmem] * count + [hbm] + [anywhere] * len(after),
        out_specs=[vmem] * count,
        scratch_shapes=[
            pltpu.VMEM((count, BLK, HD), jnp.bfloat16),
            pltpu.VMEM((count, BLK, HD), jnp.bfloat16),
            pltpu.SemaphoreType.DMA((2, count)),
        ],
        compiler_params=params(),
        cost_estimate=pl.CostEstimate(flops=1 << 36, bytes_accessed=1 << 30, transcendentals=1),
        name="serve_slots",
    )(*slots, kv_cache, *after)


def serve_group_kernel(me_ref, slots_ref, kv_ref, *refs):
    out_ref, keys, values, sems = refs[-4:]
    own_place = me_ref[0] & (NEAR - 1)
    copies = []
    for index in range(NEAR - 1):
        place = own_place ^ (index + 1)
        number = jnp.max(slots_ref[place, ROWS:SLOT, :].astype(jnp.float32)).astype(jnp.int32)
        start = pl.multiple_of(number * BLK, BLK)
        for half, buffer in enumerate((keys, values)):
            copy = pltpu.make_async_copy(
                kv_ref.at[half, pl.ds(start, BLK)], buffer.at[index], sems.at[half, index]
            )
            copy.start()
            copies.append(copy)
    out_ref[own_place] = jnp.zeros((SLOT, HD), jnp.bfloat16)
    for index in range(NEAR - 1):
        place = own_place ^ (index + 1)
        copies[2 * index].wait()
        copies[2 * index + 1].wait()
        attend(slots_ref[place, 0:ROWS, :], keys[index], values[index], None, out_ref.at[place])


def serve_group(me, slots, kv_cache, after):
    return pl.pallas_call(
        serve_group_kernel,
        out_shape=jax.ShapeDtypeStruct((NEAR, SLOT, HD), jnp.bfloat16),
        in_specs=[smem, vmem, hbm] + [anywhere] * len(after),
        out_specs=vmem,
        scratch_shapes=[
            pltpu.VMEM((NEAR - 1, BLK, HD), jnp.bfloat16),
            pltpu.VMEM((NEAR - 1, BLK, HD), jnp.bfloat16),
            pltpu.SemaphoreType.DMA((2, NEAR - 1)),
        ],
        compiler_params=params(),
        cost_estimate=pl.CostEstimate(flops=1 << 36, bytes_accessed=1 << 30, transcendentals=1),
        name="serve_group",
    )(me, slots, kv_cache, *after)


def levels_of(parts):
    parts = parts.astype(jnp.float32)
    return parts[0:GROUP] + parts[GROUP : 2 * GROUP] + parts[2 * GROUP : 3 * GROUP]


def combine_kernel(
    tiles, blocks, seq_count, me_ref, selected_ref, own_ref, self_ref, near_ref, *refs
):
    far_refs, out_ref, blend = refs[: seq_count - NEAR], refs[-2], refs[-1]
    own_place = me_ref[0] & (NEAR - 1)
    slots = [self_ref, *[near_ref.at[own_place ^ offset] for offset in range(1, NEAR)], *far_refs]
    routes = [
        route(selected_ref, me_ref[0], me_ref[0] ^ offset, tiles, blocks)
        for offset in range(seq_count)
    ]
    slot_levels = [levels_of(slot[ROWS:SLOT, :]) for slot in slots]
    for tile in range(tiles):
        own_level = levels_of(own_ref[tile, ROWS:SLOT, :])
        mine = [(filled > 0) & (number == tile) for number, _, filled in routes]
        levels = [own_level] + [
            jnp.where(used, level, -jnp.inf) for used, level in zip(mine, slot_levels)
        ]
        highest = functools.reduce(jnp.maximum, levels)
        factors = [jnp.exp(level - highest) for level in levels]
        norm = functools.reduce(jnp.add, factors)
        lines = jnp.concatenate([factor / norm for factor in factors], axis=0)
        count = lines.shape[0]
        room = -count % TILE
        if room:
            lines = jnp.concatenate([lines, jnp.zeros((room, TILE), jnp.float32)], axis=0)
        columns = jnp.concatenate(
            [lines[part * TILE : (part + 1) * TILE].T for part in range(lines.shape[0] // TILE)],
            axis=1,
        )
        for head in range(GROUP):
            part = slice(head * TILE, (head + 1) * TILE)
            blend[part, :] = columns[:, head : head + 1] * own_ref[tile, part, :].astype(jnp.float32)
        for index, used in enumerate(mine):

            @pl.when(used)
            def _(index=index, columns=columns):
                for head in range(GROUP):
                    part = slice(head * TILE, (head + 1) * TILE)
                    column = (index + 1) * GROUP + head
                    blend[part, :] += columns[:, column : column + 1] * slots[index][part, :].astype(
                        jnp.float32
                    )

        for head in range(GROUP):
            out_ref[tile * TILE : (tile + 1) * TILE, head * HD : (head + 1) * HD] = blend[
                head * TILE : (head + 1) * TILE, :
            ].astype(jnp.bfloat16)


def combine(me, selected, own, self_answer, near, far, blocks, after):
    tiles, seq_count = own.shape[0], NEAR + len(far)
    return pl.pallas_call(
        functools.partial(combine_kernel, tiles, blocks, seq_count),
        out_shape=jax.ShapeDtypeStruct((tiles * TILE, GROUP * HD), jnp.bfloat16),
        in_specs=[smem, smem, vmem, vmem, vmem] + [vmem] * len(far) + [anywhere] * len(after),
        out_specs=vmem,
        scratch_shapes=[pltpu.VMEM((ROWS, HD), jnp.float32)],
        compiler_params=params(),
        cost_estimate=pl.CostEstimate(flops=1 << 36, bytes_accessed=1 << 30, transcendentals=1),
        name="combine_pieces",
    )(me, selected, own, self_answer, near, *far, *after)


def halves(numbers_ref, first, second):
    even = ((numbers_ref[0] ^ numbers_ref[2]) & 1) == 0
    return jnp.where(even, first, second), jnp.where(even, second, first)


def project_kernel(numbers_ref, own_ref, core_ref, stack, stack_z, stack_x, whole_ref, share_ref):
    depth = own_ref.shape[1]
    part = lax.shift_right_logical(numbers_ref[0] ^ numbers_ref[2], 1)
    rows = pl.ds(pl.multiple_of(part * depth, depth), depth)
    even, odd = halves(numbers_ref, own_ref[...], core_ref[...])
    whole_ref[...] = jnp.dot(even, stack[rows, :], preferred_element_type=jnp.float32) + jnp.dot(
        odd, stack_z[rows, :], preferred_element_type=jnp.float32
    )
    share_ref[...] = jnp.dot(even, stack_x[rows, :], preferred_element_type=jnp.float32)


def finish_kernel(numbers_ref, own_ref, core_ref, y_ref, both_ref, *refs):
    stack, stack_z, stack_x, first_ref, second_ref, whole_ref, share_ref, out_ref = refs
    depth, width = first_ref.shape
    x = numbers_ref[1]
    part = lax.shift_right_logical(numbers_ref[0] ^ numbers_ref[2], 1)
    rows = pl.ds(pl.multiple_of((1 - part) * depth, depth), depth)
    _, near_odd = halves(numbers_ref, own_ref[...], core_ref[...])
    even, odd = halves(numbers_ref, y_ref[...], both_ref[...])
    whole = (
        whole_ref[...]
        + jnp.dot(even, stack[rows, :], preferred_element_type=jnp.float32)
        + jnp.dot(odd, stack_z[rows, :], preferred_element_type=jnp.float32)
    )
    share = (
        share_ref[...]
        + jnp.dot(even, stack_x[rows, :], preferred_element_type=jnp.float32)
        + jnp.dot(
            jnp.where(part == 0, near_odd, odd), first_ref[...], preferred_element_type=jnp.float32
        )
        + jnp.dot(
            jnp.where(part == 0, odd, near_odd), second_ref[...], preferred_element_type=jnp.float32
        )
    )
    out_ref[:, pl.ds(pl.multiple_of(x * width, width), width)] = whole.astype(jnp.bfloat16)
    out_ref[:, pl.ds(pl.multiple_of((x ^ 1) * width, width), width)] = share.astype(jnp.bfloat16)


def project(numbers, attentions, stacks):
    rows, width = attentions[0].shape[0], stacks[0].shape[1]
    return pl.pallas_call(
        project_kernel,
        out_shape=[jax.ShapeDtypeStruct((rows, width), jnp.float32)] * 2,
        in_specs=[smem] + [vmem] * 5,
        out_specs=[vmem] * 2,
        compiler_params=params(),
        name="project",
    )(numbers, *attentions, *stacks)


def finish(numbers, attentions, stacks, whole, share):
    rows, width = attentions[0].shape[0], stacks[0].shape[1]
    return pl.pallas_call(
        finish_kernel,
        out_shape=jax.ShapeDtypeStruct((rows, 2 * width), jnp.bfloat16),
        in_specs=[smem] + [vmem] * 11,
        out_specs=vmem,
        compiler_params=params(),
        name="finish",
    )(numbers, *attentions, *stacks, whole, share)


def gate_kernel(*refs):
    del refs


def gate(array, *after):
    return pl.pallas_call(
        gate_kernel,
        out_shape=jax.ShapeDtypeStruct(array.shape, array.dtype),
        in_specs=[anywhere] * (1 + len(after)),
        out_specs=anywhere,
        input_output_aliases={0: 0},
        compiler_params=params(),
        cost_estimate=pl.CostEstimate(flops=1 << 36, bytes_accessed=1 << 30, transcendentals=1),
        name="gate",
    )(array, *after)


def pairs(count, offset):
    return [(index, index ^ offset) for index in range(count)]


def jump(weight, kvh_count, flip):
    moves = []
    for z in range(kvh_count):
        for x in range(2):
            for h in range(kvh_count):
                moves.append(((z * 2 + x) * kvh_count + h, ((h ^ flip) * 2 + x) * kvh_count + z))
    return lax.ppermute(weight, ("seq", "kvh"), moves)


def per_device(queries, kv_cache, selected, out_weight):
    seq_count, kvh_count = lax.axis_size("seq"), lax.axis_size("kvh")
    seq, kvh = lax.axis_index("seq"), lax.axis_index("kvh")
    blocks = kv_cache.shape[1] // BLK
    me = seq.astype(jnp.int32).reshape(1)
    requests = selected
    fast = seq_count == 2 * kvh_count and kvh_count == 4

    def move(array, offset):
        return lax.ppermute(array, "seq", pairs(seq_count, offset))

    stack = stack_z = stack_x = None
    if fast:
        jumps = [jump(out_weight, kvh_count, 0), jump(out_weight, kvh_count, 2)]
    if fast:
        stack = jnp.concatenate(jumps, axis=0)
        stack_z = move(stack, 2)
        stack_x = move(stack, 1)
    groups = [list(range(base, base + NEAR)) for base in range(0, seq_count, NEAR)]

    def swap(array):
        return lax.all_to_all(
            array, "seq", split_axis=0, concat_axis=0, axis_index_groups=groups, tiled=True
        )

    near, mine, *far = pack(me, requests, queries, seq_count, blocks)
    arrived = {NEAR + index: move(slot, NEAR + index) for index, slot in enumerate(far)}
    returned = {}

    def answer(offsets, after):
        answers = serve([arrived[offset] for offset in offsets], kv_cache, after)
        for offset, result in zip(offsets, answers):
            returned[offset] = move(result, offset)
        return answers[-1]

    own = own_pieces(queries, kv_cache, [near])
    near_answers = serve_group(me, swap(near), kv_cache, [own] + [])
    returned_near = swap(near_answers)
    half = (seq_count + NEAR) // 2
    self_answer = serve([mine], kv_cache, [own] + ([stack] if fast else []))[0]
    first = answer(list(range(NEAR, half)), [self_answer] + ([stack] if fast else []))
    last = answer(list(range(half, seq_count)), [first] + [])
    if fast:
        depth = out_weight.shape[0]
        first_zx = move(gate(stack_z[:depth], last), 1)
        second_zx = move(gate(stack_x[depth:], last), 2)
    tick = gate(last, returned_near, *[returned[offset] for offset in range(NEAR, half)], *([stack_x] if fast else []))
    far = [returned[offset] for offset in range(NEAR, seq_count)]
    attention = combine(me, requests, own, self_answer, returned_near, far, blocks, [tick] + [])
    if fast:
        other_y = lax.ppermute(attention, "kvh", pairs(kvh_count, 2))
        other_core = lax.ppermute(attention, "kvh", pairs(kvh_count, 1))
        numbers = jnp.stack([lax.shift_right_logical(seq, 1), seq & 1, kvh]).astype(jnp.int32)
        stacks = [stack, stack_z, stack_x]
        whole, share = project(numbers, [attention, other_core], stacks)
        other_y = gate(other_y, whole, first_zx, second_zx)
        both = lax.ppermute(other_y, "kvh", pairs(kvh_count, 1))
        attentions = [attention, other_core, other_y, both]
        return finish(numbers, attentions, [*stacks, first_zx, second_zx], whole, share)
    column_terms = jnp.dot(
        attention,
        lax.all_gather(out_weight, "seq", axis=1, tiled=True),
        preferred_element_type=jnp.float32,
    )
    return lax.psum_scatter(
        column_terms.astype(jnp.bfloat16), "kvh", scatter_dimension=1, tiled=True
    )


def solution(mesh):
    in_specs = (P("seq", "kvh"), P(None, "seq", "kvh"), P("seq", "kvh", None), P("kvh", "seq"))
    out_specs = P("seq", "kvh")
    return jax.shard_map(
        per_device, mesh=mesh, in_specs=in_specs, out_specs=out_specs, check_vma=False
    )
```

```python
import functools
import math

import jax
import jax.numpy as jnp
from jax import lax
from jax.experimental import pallas as pl
from jax.experimental.pallas import tpu as pltpu
from jax.sharding import PartitionSpec as P

GROUP = 4
HD = 128
BLK = 1024
TILE = 128
SEL = 2
ROWS = GROUP * TILE
SLOT = ROWS + 16
NEAR = 4
SCALE = HD ** (-0.5)
LOG2E = math.log2(math.e)
VMEM_LIMIT = 48 * 1024 * 1024

vmem = pl.BlockSpec(memory_space=pltpu.VMEM)
smem = pl.BlockSpec(memory_space=pltpu.SMEM)
hbm = pl.BlockSpec(memory_space=pltpu.HBM)
anywhere = pl.BlockSpec(memory_space=pl.ANY)


def params():
    return pltpu.CompilerParams(vmem_limit_bytes=VMEM_LIMIT)


def route(selected_ref, own_seq, peer, tiles, blocks):
    own_block = own_seq * blocks + blocks - 1
    tile, block, filled = jnp.int32(0), jnp.int32(0), jnp.int32(0)
    for request in range(tiles * SEL):
        chosen = selected_ref[request // SEL, 0, request % SEL]
        target = jnp.where(chosen >= own_block, chosen + 1, chosen)
        here = lax.div(target, jnp.int32(blocks)) == peer
        tile = jnp.where(here, request // SEL, tile)
        block = jnp.where(here, lax.rem(target, jnp.int32(blocks)), block)
        filled = jnp.where(here, 1, filled)
    return tile, block, filled


def pack_kernel(tiles, blocks, me_ref, selected_ref, query_ref, near_ref, *far_refs):
    def fill(slot, peer):
        tile, block, _ = route(selected_ref, me_ref[0], peer, tiles, blocks)
        rows = pl.ds(pl.multiple_of(tile * TILE, TILE), TILE)
        for head in range(GROUP):
            slot[head * TILE : (head + 1) * TILE, :] = query_ref[rows, head * HD : (head + 1) * HD]
        slot[ROWS:SLOT, :] = jnp.full((16, HD), block.astype(jnp.float32)).astype(jnp.bfloat16)

    for place in range(NEAR):
        fill(near_ref.at[place], (me_ref[0] & ~(NEAR - 1)) + place)
    for index, slot in enumerate(far_refs):
        fill(slot, me_ref[0] ^ (NEAR + index))


def pack(me, selected, queries, seq_count, blocks):
    tiles = queries.shape[0] // TILE
    return pl.pallas_call(
        functools.partial(pack_kernel, tiles, blocks),
        out_shape=[jax.ShapeDtypeStruct((NEAR, SLOT, HD), jnp.bfloat16)]
        + [jax.ShapeDtypeStruct((SLOT, HD), jnp.bfloat16)] * (seq_count - NEAR),
        in_specs=[smem, smem, vmem],
        out_specs=[vmem] * (seq_count - NEAR + 1),
        compiler_params=params(),
        name="pack_queries",
    )(me, selected, queries)


def attend(query, keys, values, first_offset, out_ref):
    levels = []
    step = ROWS // 2
    for base in range(0, ROWS, step):
        scores = lax.dot_general(
            query[base : base + step], keys, (((1,), (1,)), ((), ())), preferred_element_type=jnp.float32
        )
        if first_offset is not None:
            offsets = first_offset + lax.rem(
                lax.broadcasted_iota(jnp.int32, (step, BLK), 0), jnp.int32(TILE)
            )
            seen = lax.broadcasted_iota(jnp.int32, (step, BLK), 1) <= offsets
            scores = jnp.where(seen, scores, -jnp.inf)
        top = jnp.max(scores, axis=1, keepdims=True)
        weights = jnp.exp2((scores - top) * (SCALE * LOG2E))
        total = jnp.sum(weights, axis=1, keepdims=True)
        summed = jnp.dot(weights.astype(jnp.bfloat16), values, preferred_element_type=jnp.float32)
        out_ref[base : base + step, :] = (summed / total).astype(jnp.bfloat16)
        levels.append(top * SCALE + jnp.log(total))
    level = jnp.concatenate(levels, axis=0)
    lane = lax.rem(lax.broadcasted_iota(jnp.int32, (TILE, TILE), 1), jnp.int32(GROUP))
    spread = jnp.zeros((TILE, TILE), jnp.float32)
    for head in range(GROUP):
        spread = jnp.where(lane == head, level[head * TILE : (head + 1) * TILE], spread)
    lines = spread.T[0:16]
    high = lines.astype(jnp.bfloat16).astype(jnp.float32)
    middle = (lines - high).astype(jnp.bfloat16).astype(jnp.float32)
    low = lines - high - middle
    row = lax.broadcasted_iota(jnp.int32, (16, TILE), 0)
    parts = jnp.where(row < GROUP, high, jnp.where(row < 2 * GROUP, middle, low))
    out_ref[ROWS:SLOT, :] = parts.astype(jnp.bfloat16)


def own_kernel(tiles, blocks, query_ref, kv_ref, *refs):
    out_ref, keys, values, sems = refs[-4:]
    start = (blocks - 1) * BLK
    copies = [
        pltpu.make_async_copy(kv_ref.at[0, pl.ds(start, BLK)], keys, sems.at[0]),
        pltpu.make_async_copy(kv_ref.at[1, pl.ds(start, BLK)], values, sems.at[1]),
    ]
    for copy in copies:
        copy.start()
    for copy in copies:
        copy.wait()

    def one(tile, carry):
        rows = pl.ds(pl.multiple_of(tile * TILE, TILE), TILE)
        query = jnp.concatenate(
            [query_ref[rows, head * HD : (head + 1) * HD] for head in range(GROUP)], axis=0
        )
        first_offset = BLK - tiles * TILE + tile * TILE
        attend(query, keys[...], values[...], first_offset, out_ref.at[tile])
        return carry

    lax.fori_loop(0, tiles, one, 0)


def own_pieces(queries, kv_cache, after):
    tiles, blocks = queries.shape[0] // TILE, kv_cache.shape[1] // BLK
    return pl.pallas_call(
        functools.partial(own_kernel, tiles, blocks),
        out_shape=jax.ShapeDtypeStruct((tiles, SLOT, HD), jnp.bfloat16),
        in_specs=[vmem, hbm] + [anywhere] * len(after),
        out_specs=vmem,
        scratch_shapes=[
            pltpu.VMEM((BLK, HD), jnp.bfloat16),
            pltpu.VMEM((BLK, HD), jnp.bfloat16),
            pltpu.SemaphoreType.DMA((2,)),
        ],
        compiler_params=params(),
        cost_estimate=pl.CostEstimate(flops=1 << 36, bytes_accessed=1 << 30, transcendentals=1),
        name="own_pieces",
    )(queries, kv_cache, *after)


def serve_kernel(count, *refs):
    slots, kv_ref, outs = refs[:count], refs[count], refs[-count - 3 : -3]
    keys, values, sems = refs[-3:]
    copies = []
    for index, slot in enumerate(slots):
        number = jnp.max(slot[ROWS:SLOT, :].astype(jnp.float32)).astype(jnp.int32)
        start = pl.multiple_of(number * BLK, BLK)
        for half, buffer in enumerate((keys, values)):
            copy = pltpu.make_async_copy(
                kv_ref.at[half, pl.ds(start, BLK)], buffer.at[index], sems.at[half, index]
            )
            copy.start()
            copies.append(copy)
    for index, slot in enumerate(slots):
        copies[2 * index].wait()
        copies[2 * index + 1].wait()
        attend(slot[0:ROWS, :], keys[index], values[index], None, outs[index])


def serve(slots, kv_cache, after):
    count = len(slots)
    return pl.pallas_call(
        functools.partial(serve_kernel, count),
        out_shape=[jax.ShapeDtypeStruct((SLOT, HD), jnp.bfloat16)] * count,
        in_specs=[vmem] * count + [hbm] + [anywhere] * len(after),
        out_specs=[vmem] * count,
        scratch_shapes=[
            pltpu.VMEM((count, BLK, HD), jnp.bfloat16),
            pltpu.VMEM((count, BLK, HD), jnp.bfloat16),
            pltpu.SemaphoreType.DMA((2, count)),
        ],
        compiler_params=params(),
        cost_estimate=pl.CostEstimate(flops=1 << 36, bytes_accessed=1 << 30, transcendentals=1),
        name="serve_slots",
    )(*slots, kv_cache, *after)


def serve_group_kernel(slots_ref, kv_ref, *refs):
    out_ref, keys, values, sems = refs[-4:]
    copies = []
    for place in range(NEAR):
        number = jnp.max(slots_ref[place, ROWS:SLOT, :].astype(jnp.float32)).astype(jnp.int32)
        start = pl.multiple_of(number * BLK, BLK)
        for half, buffer in enumerate((keys, values)):
            copy = pltpu.make_async_copy(
                kv_ref.at[half, pl.ds(start, BLK)], buffer.at[place], sems.at[half, place]
            )
            copy.start()
            copies.append(copy)
    for place in range(NEAR):
        copies[2 * place].wait()
        copies[2 * place + 1].wait()
        attend(slots_ref[place, 0:ROWS, :], keys[place], values[place], None, out_ref.at[place])


def serve_group(slots, kv_cache, after):
    return pl.pallas_call(
        serve_group_kernel,
        out_shape=jax.ShapeDtypeStruct((NEAR, SLOT, HD), jnp.bfloat16),
        in_specs=[vmem, hbm] + [anywhere] * len(after),
        out_specs=vmem,
        scratch_shapes=[
            pltpu.VMEM((NEAR, BLK, HD), jnp.bfloat16),
            pltpu.VMEM((NEAR, BLK, HD), jnp.bfloat16),
            pltpu.SemaphoreType.DMA((2, NEAR)),
        ],
        compiler_params=params(),
        cost_estimate=pl.CostEstimate(flops=1 << 36, bytes_accessed=1 << 30, transcendentals=1),
        name="serve_group",
    )(slots, kv_cache, *after)


def levels_of(parts):
    parts = parts.astype(jnp.float32)
    return parts[0:GROUP] + parts[GROUP : 2 * GROUP] + parts[2 * GROUP : 3 * GROUP]


def combine_kernel(tiles, blocks, seq_count, me_ref, selected_ref, own_ref, near_ref, *refs):
    far_refs, out_ref, blend = refs[: seq_count - NEAR], refs[-2], refs[-1]
    slots, routes = [], []
    for place in range(NEAR):
        slots.append(near_ref.at[place])
        routes.append(
            route(selected_ref, me_ref[0], (me_ref[0] & ~(NEAR - 1)) + place, tiles, blocks)
        )
    for index, slot in enumerate(far_refs):
        slots.append(slot)
        routes.append(route(selected_ref, me_ref[0], me_ref[0] ^ (NEAR + index), tiles, blocks))
    slot_levels = [levels_of(slot[ROWS:SLOT, :]) for slot in slots]
    for tile in range(tiles):
        own_level = levels_of(own_ref[tile, ROWS:SLOT, :])
        mine = [(filled > 0) & (number == tile) for number, _, filled in routes]
        levels = [own_level] + [
            jnp.where(used, level, -jnp.inf) for used, level in zip(mine, slot_levels)
        ]
        highest = functools.reduce(jnp.maximum, levels)
        factors = [jnp.exp(level - highest) for level in levels]
        norm = functools.reduce(jnp.add, factors)
        lines = jnp.concatenate([factor / norm for factor in factors], axis=0)
        count = lines.shape[0]
        room = -count % TILE
        if room:
            lines = jnp.concatenate([lines, jnp.zeros((room, TILE), jnp.float32)], axis=0)
        columns = jnp.concatenate(
            [lines[part * TILE : (part + 1) * TILE].T for part in range(lines.shape[0] // TILE)],
            axis=1,
        )
        for head in range(GROUP):
            part = slice(head * TILE, (head + 1) * TILE)
            blend[part, :] = columns[:, head : head + 1] * own_ref[tile, part, :].astype(jnp.float32)
        for index, used in enumerate(mine):

            @pl.when(used)
            def _(index=index, columns=columns):
                for head in range(GROUP):
                    part = slice(head * TILE, (head + 1) * TILE)
                    column = (index + 1) * GROUP + head
                    blend[part, :] += columns[:, column : column + 1] * slots[index][part, :].astype(
                        jnp.float32
                    )

        for head in range(GROUP):
            out_ref[tile * TILE : (tile + 1) * TILE, head * HD : (head + 1) * HD] = blend[
                head * TILE : (head + 1) * TILE, :
            ].astype(jnp.bfloat16)


def combine(me, selected, own, near, far, blocks, after):
    tiles, seq_count = own.shape[0], NEAR + len(far)
    return pl.pallas_call(
        functools.partial(combine_kernel, tiles, blocks, seq_count),
        out_shape=jax.ShapeDtypeStruct((tiles * TILE, GROUP * HD), jnp.bfloat16),
        in_specs=[smem, smem, vmem, vmem] + [vmem] * len(far) + [anywhere] * len(after),
        out_specs=vmem,
        scratch_shapes=[pltpu.VMEM((ROWS, HD), jnp.float32)],
        compiler_params=params(),
        cost_estimate=pl.CostEstimate(flops=1 << 36, bytes_accessed=1 << 30, transcendentals=1),
        name="combine_pieces",
    )(me, selected, own, near, *far, *after)


def halves(numbers_ref, first, second):
    even = ((numbers_ref[0] ^ numbers_ref[2]) & 1) == 0
    return jnp.where(even, first, second), jnp.where(even, second, first)


def project_kernel(numbers_ref, own_ref, core_ref, stack, stack_z, stack_x, whole_ref, share_ref):
    depth = own_ref.shape[1]
    part = lax.shift_right_logical(numbers_ref[0] ^ numbers_ref[2], 1)
    rows = pl.ds(pl.multiple_of(part * depth, depth), depth)
    even, odd = halves(numbers_ref, own_ref[...], core_ref[...])
    whole_ref[...] = jnp.dot(even, stack[rows, :], preferred_element_type=jnp.float32) + jnp.dot(
        odd, stack_z[rows, :], preferred_element_type=jnp.float32
    )
    share_ref[...] = jnp.dot(even, stack_x[rows, :], preferred_element_type=jnp.float32)


def finish_kernel(numbers_ref, own_ref, core_ref, y_ref, both_ref, *refs):
    stack, stack_z, stack_x, first_ref, second_ref, whole_ref, share_ref, out_ref = refs
    depth, width = first_ref.shape
    x = numbers_ref[1]
    part = lax.shift_right_logical(numbers_ref[0] ^ numbers_ref[2], 1)
    rows = pl.ds(pl.multiple_of((1 - part) * depth, depth), depth)
    _, near_odd = halves(numbers_ref, own_ref[...], core_ref[...])
    even, odd = halves(numbers_ref, y_ref[...], both_ref[...])
    last = [jnp.where(part == 0, near_odd, odd), jnp.where(part == 0, odd, near_odd)]
    whole = whole_ref[...] + jnp.dot(
        jnp.concatenate([even, odd], axis=1),
        jnp.concatenate([stack[rows, :], stack_z[rows, :]], axis=0),
        preferred_element_type=jnp.float32,
    )
    share = share_ref[...] + jnp.dot(
        jnp.concatenate([even, *last], axis=1),
        jnp.concatenate([stack_x[rows, :], first_ref[...], second_ref[...]], axis=0),
        preferred_element_type=jnp.float32,
    )
    out_ref[:, pl.ds(pl.multiple_of(x * width, width), width)] = whole.astype(jnp.bfloat16)
    out_ref[:, pl.ds(pl.multiple_of((x ^ 1) * width, width), width)] = share.astype(jnp.bfloat16)


def project(numbers, attentions, stacks):
    rows, width = attentions[0].shape[0], stacks[0].shape[1]
    return pl.pallas_call(
        project_kernel,
        out_shape=[jax.ShapeDtypeStruct((rows, width), jnp.float32)] * 2,
        in_specs=[smem] + [vmem] * 5,
        out_specs=[vmem] * 2,
        compiler_params=params(),
        name="project",
    )(numbers, *attentions, *stacks)


def finish(numbers, attentions, stacks, whole, share):
    rows, width = attentions[0].shape[0], stacks[0].shape[1]
    return pl.pallas_call(
        finish_kernel,
        out_shape=jax.ShapeDtypeStruct((rows, 2 * width), jnp.bfloat16),
        in_specs=[smem] + [vmem] * 11,
        out_specs=vmem,
        compiler_params=params(),
        name="finish",
    )(numbers, *attentions, *stacks, whole, share)


def gate_kernel(*refs):
    del refs


def gate(array, *after):
    return pl.pallas_call(
        gate_kernel,
        out_shape=jax.ShapeDtypeStruct(array.shape, array.dtype),
        in_specs=[anywhere] * (1 + len(after)),
        out_specs=anywhere,
        input_output_aliases={0: 0},
        compiler_params=params(),
        cost_estimate=pl.CostEstimate(flops=1 << 36, bytes_accessed=1 << 30, transcendentals=1),
        name="gate",
    )(array, *after)


def pairs(count, offset):
    return [(index, index ^ offset) for index in range(count)]


def jump(weight, kvh_count, flip):
    moves = []
    for z in range(kvh_count):
        for x in range(2):
            for h in range(kvh_count):
                moves.append(((z * 2 + x) * kvh_count + h, ((h ^ flip) * 2 + x) * kvh_count + z))
    return lax.ppermute(weight, ("seq", "kvh"), moves)


def per_device(queries, kv_cache, selected, out_weight):
    seq_count, kvh_count = lax.axis_size("seq"), lax.axis_size("kvh")
    seq, kvh = lax.axis_index("seq"), lax.axis_index("kvh")
    blocks = kv_cache.shape[1] // BLK
    me = seq.astype(jnp.int32).reshape(1)
    requests = selected
    fast = seq_count == 2 * kvh_count and kvh_count == 4

    def move(array, offset):
        return lax.ppermute(array, "seq", pairs(seq_count, offset))

    stack = stack_z = stack_x = None
    if fast:
        jumps = [jump(out_weight, kvh_count, 0), jump(out_weight, kvh_count, 2)]
    if fast:
        stack = jnp.concatenate(jumps, axis=0)
        stack_z = move(stack, 2)
        stack_x = move(stack, 1)
    groups = [list(range(base, base + NEAR)) for base in range(0, seq_count, NEAR)]

    def swap(array):
        return lax.all_to_all(
            array, "seq", split_axis=0, concat_axis=0, axis_index_groups=groups, tiled=True
        )

    near, *far = pack(me, requests, queries, seq_count, blocks)
    arrived = {NEAR + index: move(slot, NEAR + index) for index, slot in enumerate(far)}
    returned = {}

    def answer(offsets, after):
        answers = serve([arrived[offset] for offset in offsets], kv_cache, after)
        for offset, result in zip(offsets, answers):
            returned[offset] = move(result, offset)
        return answers[-1]

    own = own_pieces(queries, kv_cache, [near])
    near_answers = serve_group(swap(near), kv_cache, [own] + [])
    returned_near = swap(near_answers)
    half = (seq_count + NEAR) // 2
    first = answer(list(range(NEAR, half)), [own] + ([stack] if fast else []))
    last = answer(list(range(half, seq_count)), [first] + [])
    if fast:
        depth = out_weight.shape[0]
        first_zx = move(gate(stack_z[:depth], near_answers), 1)
        second_zx = move(gate(stack_x[depth:], near_answers), 2)
    tick = gate(last, returned_near, *[returned[offset] for offset in range(NEAR, half)], *([stack_x] if fast else []))
    far = [returned[offset] for offset in range(NEAR, seq_count)]
    attention = combine(me, requests, own, returned_near, far, blocks, [tick] + [])
    if fast:
        other_y = lax.ppermute(attention, "kvh", pairs(kvh_count, 2))
        other_core = lax.ppermute(attention, "kvh", pairs(kvh_count, 1))
        numbers = jnp.stack([lax.shift_right_logical(seq, 1), seq & 1, kvh]).astype(jnp.int32)
        stacks = [stack, stack_z, stack_x]
        whole, share = project(numbers, [attention, other_core], stacks)
        other_y = gate(other_y, whole, first_zx, second_zx)
        both = lax.ppermute(other_y, "kvh", pairs(kvh_count, 1))
        attentions = [attention, other_core, other_y, both]
        return finish(numbers, attentions, [*stacks, first_zx, second_zx], whole, share)
    column_terms = jnp.dot(
        attention,
        lax.all_gather(out_weight, "seq", axis=1, tiled=True),
        preferred_element_type=jnp.float32,
    )
    return lax.psum_scatter(
        column_terms.astype(jnp.bfloat16), "kvh", scatter_dimension=1, tiled=True
    )


def solution(mesh):
    in_specs = (P("seq", "kvh"), P(None, "seq", "kvh"), P("seq", "kvh", None), P("kvh", "seq"))
    out_specs = P("seq", "kvh")
    return jax.shard_map(
        per_device, mesh=mesh, in_specs=in_specs, out_specs=out_specs, check_vma=False
    )
```
